256 devices in a mesh: seq: 16 (over z_lo, y, core), fsdp: 16 (over x, z_hi).
Axes of the slice: x: 4, y: 4, z: 8 (z_hi: 4, z_lo: 2; z = z_hi * 2 + z_lo), core: 2. Of those that a mesh axis runs over, the one named last changes fastest.
Arguments:
- activations: bfloat16 [16, 4096, 1536], P('fsdp', 'seq'), may hold values from -64 to 64, as said below
- query_weight: bfloat16 [1536, 512], P('fsdp'), may hold values from -1 to 1
- key_weight: bfloat16 [1536, 128], P('fsdp'), may hold values from -1 to 1
- value_weight: bfloat16 [1536, 128], P('fsdp'), may hold values from -0.15625 to 0.15625
- output_weight: bfloat16 [512, 1536], P('fsdp'), may hold values from -0.25 to 0.25
- cotangent: bfloat16 [16, 4096, 1536], P('fsdp', 'seq'), may hold values from -6 to 6
Outputs:
- layer_out: bfloat16 [16, 4096, 1536], P('fsdp', 'seq')
- input_grad: bfloat16 [16, 4096, 1536], P('fsdp', 'seq')
- query_grad: float32 [1536, 512], P('fsdp')
- key_grad: float32 [1536, 128], P('fsdp')
- value_grad: float32 [1536, 128], P('fsdp')
- output_grad: float32 [512, 1536], P('fsdp')
The draws below stay inside these ranges and needn't reach their ends.
Inputs may be any that keep to these rules, and one draw needn't show every extreme that they name: activations are real-valued.
All inputs are finite; a program needn't handle non-finite values.
Results may differ from the reference program's by a relative error of at most 0.034.
The reference program's roundings to bfloat16 on the way (of `probs_b`, `attended`, `d_att` and `dscores`) count: a program that leaves them out, or rounds other values in their place, can miss the bound.
Values may be sent and summed in bfloat16 or wider, within the bound.
No kernel may reach another device: no remote copies, remote signals or barrier semaphores. Data moves between devices by JAX's collectives and lax.ppermute only.
A program may use at most 192 MiB of HBM per device.

```python
import math
import jax
import jax.numpy as jnp
from jax import lax

D = 1536
H = 4
E = 128
LENGTH = 4096
WINDOWS = 16


def shared_base(key):
    return jax.random.normal(key, (D, E), jnp.float32) / jnp.sqrt(jnp.float32(D))


def draw_activations(key, part):
    key = jax.random.fold_in(key, 11)
    first = jax.random.fold_in(key, 0)
    shape = (WINDOWS, LENGTH, D)
    rows = jnp.clip(jax.random.normal(first, shape, jnp.float32), -6.0, 6.0)
    return rows.astype(jnp.bfloat16)


def draw_query_weight(key, part):
    base = shared_base(key)
    key = jax.random.fold_in(key, 12)
    noise = jax.random.normal(key, (D, H * E), jnp.float32) / jnp.sqrt(jnp.float32(D))
    return (0.8 * jnp.tile(base, (1, H)) + 0.6 * noise).astype(jnp.bfloat16)


def draw_key_weight(key, part):
    base = shared_base(key)
    key = jax.random.fold_in(key, 13)
    noise = jax.random.normal(key, (D, E), jnp.float32) / jnp.sqrt(jnp.float32(D))
    return (0.55 * base + 0.83 * noise).astype(jnp.bfloat16)


def raised(result, stream_key, source, target, parts, factor):
    def block_of(axis_at):
        return (jnp.arange(result.shape[axis_at]) // (result.shape[axis_at] // parts)).reshape((-1,) + (1,) * (result.ndim - 1 - axis_at))

    one_side = jax.random.permutation(stream_key, parts)[block_of(target)]
    other_side = (block_of(target) + parts // 2) % parts
    return jnp.where((block_of(source) == one_side) | (block_of(source) == other_side), factor * result, result)


def block_scale(key, shape, cuts, smallest, high):
    factor_of, own = 1.0, jax.random.fold_in(key, 6)
    for dim, shards_of in cuts:
        heights = jnp.exp(jax.random.uniform(jax.random.fold_in(own, dim), (shards_of,), jnp.float32, smallest / len(cuts), high / len(cuts)))
        factor_of = factor_of * jnp.repeat(heights, shape[dim] // shards_of).reshape([-1 if axis == dim else 1 for axis in range(len(shape))])
    return factor_of


def scatter_about(key, shape, width, limit, cuts=(), held_as=jnp.bfloat16):
    level = block_scale(key, shape, cuts, -0.22, 0.18) if cuts else 1.0
    values = jax.random.normal(key, shape, jnp.float32) * width * level
    return jnp.minimum(jnp.maximum(values, -limit), limit).astype(held_as)


def gaussian_with(rng, dims, deviation, reach, cuts, heavy, dtype=jnp.bfloat16):
    entries = deviation * jax.random.normal(rng, dims, jnp.float32)
    if cuts:
        entries = entries * block_scale(rng, dims, cuts, -0.22, 0.18)
    return jnp.clip(raised(entries, jax.random.fold_in(rng, 3), *heavy), -reach, reach).astype(dtype)


def setup_inputs(seed: int = 0) -> dict:
    streams_of = jax.random.split(jax.random.key(seed), 7)
    return {
        "activations": draw_activations(jax.random.fold_in(streams_of[6], 71), 0),
        "query_weight": draw_query_weight(jax.random.fold_in(streams_of[6], 71), 0),
        "key_weight": draw_key_weight(jax.random.fold_in(streams_of[6], 71), 0),
        "value_weight": scatter_about(streams_of[3], (D, E), D ** -0.5, 0.15625, ((0, 16),)),
        "output_weight": scatter_about(streams_of[4], (H * E, D), (H * E) ** -0.5, 0.25, ((0, 16),)),
        "cotangent": gaussian_with(streams_of[5], (WINDOWS, LENGTH, D), 1.0, 6.0, ((0, 16), (1, 16)), (1, 2, 16, 2.0)),
    }


def window_pass(x, g, query_weight, key_weight, value_weight, output_weight):
    length = x.shape[0]
    scale = 1.0 / math.sqrt(E)
    queries = jnp.dot(x, query_weight, preferred_element_type=jnp.float32).astype(jnp.bfloat16)
    keys = jnp.dot(x, key_weight, preferred_element_type=jnp.float32).astype(jnp.bfloat16)
    values = jnp.dot(x, value_weight, preferred_element_type=jnp.float32).astype(jnp.bfloat16)
    heads = queries.reshape(length, H, E).astype(jnp.float32)
    keys_f = keys.astype(jnp.float32)
    values_f = values.astype(jnp.float32)
    scores = jnp.einsum('qhe,ke->hqk', heads, keys_f) * scale
    probs = jax.nn.softmax(scores, axis=-1)
    probs_b = lax.optimization_barrier(probs.astype(jnp.bfloat16)).astype(jnp.float32)
    attended = jnp.einsum('hqk,ke->qhe', probs_b, values_f).reshape(length, H * E).astype(jnp.bfloat16)
    layer_out = jnp.dot(attended, output_weight, preferred_element_type=jnp.float32).astype(jnp.bfloat16)
    d_att = jnp.dot(g, output_weight.T, preferred_element_type=jnp.float32).astype(jnp.bfloat16)
    d_heads = d_att.reshape(length, H, E).astype(jnp.float32)
    dprobs = jnp.einsum('qhe,ke->hqk', d_heads, values_f)
    dscores = probs * (dprobs - lax.optimization_barrier(jnp.sum(probs * dprobs, axis=-1, keepdims=True)))
    dscores_b = lax.optimization_barrier((dscores * scale).astype(jnp.bfloat16)).astype(jnp.float32)
    d_query = jnp.einsum('hqk,ke->qhe', dscores_b, keys_f).reshape(length, H * E).astype(jnp.bfloat16)
    d_key = jnp.einsum('hqk,qhe->ke', dscores_b, heads).astype(jnp.bfloat16)
    d_value = jnp.einsum('hqk,qhe->ke', probs_b, d_heads).astype(jnp.bfloat16)
    input_grad = (jnp.dot(d_query, query_weight.T, preferred_element_type=jnp.float32) + jnp.dot(d_key, key_weight.T, preferred_element_type=jnp.float32) + jnp.dot(d_value, value_weight.T, preferred_element_type=jnp.float32)).astype(jnp.bfloat16)
    grads = (jnp.dot(x.T, d_query, preferred_element_type=jnp.float32), jnp.dot(x.T, d_key, preferred_element_type=jnp.float32), jnp.dot(x.T, d_value, preferred_element_type=jnp.float32), jnp.dot(attended.T, g, preferred_element_type=jnp.float32))
    return (layer_out, input_grad, grads)

def reference(activations, query_weight, key_weight, value_weight, output_weight, cotangent):

    def step(carry, pair):
        layer_out, input_grad, grads = window_pass(pair[0], pair[1], query_weight, key_weight, value_weight, output_weight)
        carry = tuple((a + b for a, b in zip(carry, grads)))
        return (carry, (layer_out, input_grad))
    start = (jnp.zeros((D, H * E), jnp.float32), jnp.zeros((D, E), jnp.float32), jnp.zeros((D, E), jnp.float32), jnp.zeros((H * E, D), jnp.float32))
    totals, stacked = lax.scan(step, start, (activations, cotangent))
    return (stacked[0], stacked[1], totals[0], totals[1], totals[2], totals[3])
```

```python
import math

import jax
import jax.numpy as jnp
from jax import lax
from jax.experimental import pallas as pl
from jax.experimental.pallas import tpu as pltpu
from jax.sharding import Mesh, PartitionSpec as P

f32 = jnp.float32
bf16 = jnp.bfloat16

NT = (((1,), (1,)), ((), ()))
NN = (((1,), (0,)), ((), ()))
TN = (((0,), (0,)), ((), ()))

E = 128
R = 256
C = 1024

ZL, Y, CORE, X, ZH = "zl", "y", "core", "x", "zh"
FSDP = (X, ZH)
RING = (ZL, Y)


def dot(a, b, dims):
    return lax.dot_general(a, b, dims, preferred_element_type=f32)


def attention_kernel(q_ref, k_ref, v_ref, do_ref, att_ref, dq_ref, dk_ref, dv_ref, s_ref, e_ref, acc_ref):
    length = k_ref.shape[0]
    rows, width = q_ref.shape
    scale = 1.0 / math.sqrt(E)
    scale2 = scale * math.log2(math.e)
    blocks = [(r, h) for h in range(width // E) for r in range(rows // R)]
    for n, (r, h) in enumerate(blocks):
        at = (slice(r * R, (r + 1) * R), slice(h * E, (h + 1) * E))
        q = q_ref[at]
        top = jnp.full((R, E), -jnp.inf, f32)
        for i in range(length // C):
            part = slice(i * C, (i + 1) * C)
            s = dot(q, k_ref[part, :], NT)
            s_ref[:, part] = s
            for t in range(C // E):
                top = jnp.maximum(top, s[:, t * E : (t + 1) * E])
        top = jnp.max(top, axis=1, keepdims=True) * scale2
        total = jnp.zeros((R, E), f32)
        out = jnp.zeros((R, E), f32)
        for i in range(length // C):
            part = slice(i * C, (i + 1) * C)
            e = jnp.exp2(s_ref[:, part] * scale2 - top)
            for t in range(C // E):
                total = total + e[:, t * E : (t + 1) * E]
            eb = e.astype(bf16)
            e_ref[:, part] = eb
            out = out + dot(eb, v_ref[part, :], NN)
        inverse = 1.0 / jnp.sum(total, axis=1, keepdims=True)
        out = out * inverse
        att_ref[at] = out.astype(bf16)
        do = (do_ref[at].astype(f32) * inverse).astype(bf16)
        delta = jnp.sum(do.astype(f32) * out, axis=1, keepdims=True)
        dq = jnp.zeros((R, E), f32)
        q_t = q.T
        do_t = do.T
        for i in range(length // C):
            part = slice(i * C, (i + 1) * C)
            dp = dot(do, v_ref[part, :], NT)
            eb = e_ref[:, part]
            ds = (eb.astype(f32) * (dp - delta)).astype(bf16)
            dk = dot(q_t, ds, NN)
            dv = dot(do_t, eb, NN)
            if n == 0:
                acc_ref[0:E, part] = dk
                acc_ref[E : 2 * E, part] = dv
            elif n < len(blocks) - 1:
                acc_ref[0:E, part] += dk
                acc_ref[E : 2 * E, part] += dv
            else:
                dk_ref[part, :] = ((acc_ref[0:E, part] + dk) * scale).T.astype(bf16)
                dv_ref[part, :] = (acc_ref[E : 2 * E, part] + dv).T.astype(bf16)
            dq = dq + dot(ds, k_ref[part, :], NN)
        dq_ref[at] = (dq * scale).astype(bf16)


def attention(queries, keys, values, d_att):
    rows, width = queries.shape
    length = keys.shape[0]
    vmem = pl.BlockSpec(memory_space=pltpu.VMEM)
    return pl.pallas_call(
        attention_kernel,
        out_shape=(
            jax.ShapeDtypeStruct(queries.shape, bf16),
            jax.ShapeDtypeStruct(queries.shape, bf16),
            jax.ShapeDtypeStruct(keys.shape, bf16),
            jax.ShapeDtypeStruct(keys.shape, bf16),
        ),
        in_specs=[vmem] * 4,
        out_specs=(vmem,) * 4,
        scratch_shapes=[
            pltpu.VMEM((R, length), f32),
            pltpu.VMEM((R, length), bf16),
            pltpu.VMEM((2 * E, length), f32),
        ],
        compiler_params=pltpu.CompilerParams(vmem_limit_bytes=50 * 1024 * 1024),
        cost_estimate=pl.CostEstimate(
            flops=12 * rows * length * width,
            bytes_accessed=8 * 1024 * 1024,
            transcendentals=rows * length * (width // E),
        ),
    )(queries, keys, values, d_att)


def ring_swap(value, k):
    return lax.ppermute(value, RING, [(i, i ^ k) for i in range(8)])


def core_swap(value):
    return lax.ppermute(value, CORE, [(0, 1), (1, 0)])


def shards(activations, query_weight, key_weight, value_weight, output_weight, cotangent):
    inputs = activations[0]
    upstream = cotangent[0]
    rows = inputs.shape[0]
    core = lax.axis_index(CORE)
    ring = lax.axis_index(ZL) * 4 + lax.axis_index(Y)
    first = core == 0

    both_inputs = lax.all_gather(inputs, CORE, axis=0, tiled=True)
    both_upstream = lax.all_gather(upstream, CORE, axis=0, tiled=True)

    kv_shard = jnp.where(first, key_weight, value_weight)
    q_half = lax.dynamic_slice(query_weight, (0, core * 256), (96, 256))
    q_tiles = q_half.reshape(96, 2, E).transpose(1, 0, 2).reshape(4, 48, E)
    o_half = lax.dynamic_slice(output_weight, (0, core * 768), (32, 768))
    o_tiles = o_half.reshape(32, 6, E).transpose(1, 0, 2).reshape(4, 48, E)
    tiles = jnp.concatenate([q_tiles, o_tiles], axis=0)
    piece = lax.dynamic_index_in_dim(tiles, ring, 0, keepdims=False)
    packed = jnp.concatenate([kv_shard, piece], axis=0)
    spread = lax.all_to_all(jnp.broadcast_to(packed[None], (16, 144, E)), FSDP, 0, 0)
    w_kv = spread[:, :96].reshape(1536, E)
    w_qo = lax.all_gather(spread[:, 96:], RING, axis=0)
    w_q_half = w_qo[:4].reshape(2, 2, 16, 48, E).transpose(2, 1, 3, 0, 4).reshape(1536, 256)
    w_o_half = (
        w_qo[4:].reshape(4, 16, 3, 16, E).transpose(0, 2, 1, 3, 4).reshape(6, 2, 16, 16, E)
        .transpose(2, 1, 3, 0, 4).reshape(512, 768)
    )

    kv_mine = dot(both_inputs, w_kv, NN).astype(bf16)
    kv_all = jnp.concatenate([kv_mine] + [ring_swap(kv_mine, k) for k in range(1, 8)], axis=0)
    kv_other = core_swap(kv_all)
    keys = jnp.where(first, kv_all, kv_other)
    values = jnp.where(first, kv_other, kv_all)

    w_o_other = core_swap(w_o_half)
    w_o = jnp.concatenate(
        [jnp.where(first, w_o_half, w_o_other), jnp.where(first, w_o_other, w_o_half)], axis=1
    )
    queries = dot(both_inputs, w_q_half, NN).astype(bf16)
    w_o_heads = lax.dynamic_slice(w_o, (core * 256, 0), (256, 1536))
    d_att = dot(both_upstream, w_o_heads, NT).astype(bf16)

    attended, d_query, d_keys, d_values = attention(queries, keys, values, d_att)

    kept = jnp.where(first, d_keys, d_values)
    sent = jnp.where(first, d_values, d_keys)
    d_kv = (kept.astype(f32) + core_swap(sent).astype(f32)).astype(bf16).reshape(8, 2 * rows, E)
    d_mine = d_kv[0].astype(f32)
    for k in range(1, 8):
        d_mine = d_mine + ring_swap(d_kv[k], k).astype(f32)
    d_mine = d_mine.astype(bf16)

    q_grad = dot(both_inputs, d_query, TN).astype(bf16)
    o_grad = dot(attended, both_upstream, TN).astype(bf16)
    o_kept = lax.dynamic_slice(o_grad, (0, core * 768), (256, 768))
    o_sent = lax.dynamic_slice(o_grad, (0, (1 - core) * 768), (256, 768))
    o_got = core_swap(o_sent)
    o_full = jnp.concatenate([jnp.where(first, o_kept, o_got), jnp.where(first, o_got, o_kept)], axis=0)
    q_tiles = q_grad.reshape(16, 2, 48, 2, E).transpose(3, 1, 0, 2, 4).reshape(4, 16, 48, E)
    o_tiles = (
        o_full.reshape(16, 2, 16, 6, E).transpose(3, 1, 0, 2, 4).reshape(4, 3, 16, 16, E)
        .transpose(0, 2, 1, 3, 4).reshape(4, 16, 48, E)
    )
    qo_terms = lax.psum_scatter(
        jnp.concatenate([q_tiles, o_tiles], axis=0), RING, scatter_dimension=0, tiled=False
    )

    kv_grad = dot(both_inputs, d_mine, TN).astype(bf16).reshape(16, 96, E)
    terms = lax.all_to_all(jnp.concatenate([kv_grad, qo_terms], axis=1), FSDP, 0, 0)
    share = jnp.sum(terms.astype(f32), axis=0).astype(bf16)
    spread = lax.all_to_all(jnp.broadcast_to(share[None], (8, 144, E)), RING, 0, 0)
    kv_sum = jnp.sum(spread[:, :96].astype(f32), axis=0).astype(bf16)
    final = jnp.concatenate([kv_sum, spread[:, 96:].reshape(384, E)], axis=0)
    other = core_swap(final)
    finals = [jnp.where(first, final, other), jnp.where(first, other, final)]
    key_grad, value_grad = (final[:96].astype(f32) for final in finals)
    query_grad = jnp.concatenate(
        [final[96:288].reshape(2, 96, E).transpose(1, 0, 2).reshape(96, 256) for final in finals], axis=1
    ).astype(f32)
    output_grad = jnp.concatenate(
        [final[288:].reshape(6, 32, E).transpose(1, 0, 2).reshape(32, 768) for final in finals], axis=1
    ).astype(f32)

    def own_rows(value):
        kept = lax.dynamic_slice(value, (core * rows, 0), (rows, value.shape[1]))
        got = core_swap(lax.dynamic_slice(value, ((1 - core) * rows, 0), (rows, value.shape[1])))
        return jnp.concatenate([jnp.where(first, kept, got), jnp.where(first, got, kept)], axis=1)

    layer_out = dot(own_rows(attended), w_o, NN).astype(bf16)
    w_q_other = core_swap(w_q_half)
    w_kv_other = core_swap(w_kv)
    w_q = jnp.concatenate(
        [jnp.where(first, w_q_half, w_q_other), jnp.where(first, w_q_other, w_q_half)], axis=1
    )
    w_k = jnp.where(first, w_kv, w_kv_other)
    w_v = jnp.where(first, w_kv_other, w_kv)
    d_all = jnp.concatenate([own_rows(d_query), own_rows(d_mine)], axis=1)
    w_all = jnp.concatenate([w_q, w_k, w_v], axis=1)
    input_grad = dot(d_all, w_all, NT).astype(bf16)
    return (layer_out[None], input_grad[None], query_grad, key_grad, value_grad, output_grad)


def solution(mesh):
    split = Mesh(mesh.devices.reshape(2, 4, 2, 4, 4), (ZL, Y, CORE, X, ZH))
    seq = (ZL, Y, CORE)
    return jax.shard_map(
        shards,
        mesh=split,
        in_specs=(
            P(FSDP, seq, None),
            P(FSDP, None),
            P(FSDP, None),
            P(FSDP, None),
            P(FSDP, None),
            P(FSDP, seq, None),
        ),
        out_specs=(
            P(FSDP, seq, None),
            P(FSDP, seq, None),
            P(FSDP, None),
            P(FSDP, None),
            P(FSDP, None),
            P(FSDP, None),
        ),
        check_vma=False,
    )
```

```python
import math

import jax
import jax.numpy as jnp
from jax import lax
from jax.experimental import pallas as pl
from jax.experimental.pallas import tpu as pltpu
from jax.sharding import Mesh, PartitionSpec as P

f32 = jnp.float32
bf16 = jnp.bfloat16

NT = (((1,), (1,)), ((), ()))
NN = (((1,), (0,)), ((), ()))
TN = (((0,), (0,)), ((), ()))

E = 128
R = 256
C = 1024

ZL, Y, CORE, X, ZH = "zl", "y", "core", "x", "zh"
FSDP = (X, ZH)
RING = (ZL, Y)


def dot(a, b, dims):
    return lax.dot_general(a, b, dims, preferred_element_type=f32)


def attention_kernel(
    core_ref, q_ref, mine_ref, other_ref, do_ref,
    att_ref, dq_ref, kept_ref, sent_ref,
    k_ref, v_ref, s_ref, e_ref, acc_ref,
):
    length = k_ref.shape[0]
    rows, width = q_ref.shape
    scale = 1.0 / math.sqrt(E)
    scale2 = scale * math.log2(math.e)
    first = core_ref[0] == 0

    @pl.when(first)
    def _():
        k_ref[...] = mine_ref[...]
        v_ref[...] = other_ref[...]

    @pl.when(jnp.logical_not(first))
    def _():
        k_ref[...] = other_ref[...]
        v_ref[...] = mine_ref[...]

    blocks = [(r, h) for h in range(width // E) for r in range(rows // R)]
    for n, (r, h) in enumerate(blocks):
        at = (slice(r * R, (r + 1) * R), slice(h * E, (h + 1) * E))
        q = q_ref[at]
        top = jnp.full((R, E), -jnp.inf, f32)
        for i in range(length // C):
            part = slice(i * C, (i + 1) * C)
            s = dot(q, k_ref[part, :], NT)
            s_ref[:, part] = s
            for t in range(C // E):
                top = jnp.maximum(top, s[:, t * E : (t + 1) * E])
        top = jnp.max(top, axis=1, keepdims=True) * scale2
        total = jnp.zeros((R, E), f32)
        out = jnp.zeros((R, E), f32)
        for i in range(length // C):
            part = slice(i * C, (i + 1) * C)
            e = jnp.exp2(s_ref[:, part] * scale2 - top)
            for t in range(C // E):
                total = total + e[:, t * E : (t + 1) * E]
            eb = e.astype(bf16)
            e_ref[:, part] = eb
            out = out + dot(eb, v_ref[part, :], NN)
        inverse = 1.0 / jnp.sum(total, axis=1, keepdims=True)
        out = out * inverse
        att_ref[at] = out.astype(bf16)
        do = (do_ref[at].astype(f32) * inverse).astype(bf16)
        delta = jnp.sum(do.astype(f32) * out, axis=1, keepdims=True)
        dq = jnp.zeros((R, E), f32)
        q_t = q.T
        do_t = do.T
        for i in range(length // C):
            part = slice(i * C, (i + 1) * C)
            dp = dot(do, v_ref[part, :], NT)
            eb = e_ref[:, part]
            ds = (eb.astype(f32) * (dp - delta)).astype(bf16)
            dk = dot(q_t, ds, NN)
            dv = dot(do_t, eb, NN)
            if n == 0:
                acc_ref[0:E, part] = dk
                acc_ref[E : 2 * E, part] = dv
            elif n < len(blocks) - 1:
                acc_ref[0:E, part] += dk
                acc_ref[E : 2 * E, part] += dv
            else:
                dk = (acc_ref[0:E, part] + dk) * scale
                dv = acc_ref[E : 2 * E, part] + dv
                kept_ref[part, :] = jnp.where(first, dk, dv).T.astype(bf16)
                sent_ref[part, :] = jnp.where(first, dv, dk).T.astype(bf16)
            dq = dq + dot(ds, k_ref[part, :], NN)
        dq_ref[at] = (dq * scale).astype(bf16)


def vmem_specs(n):
    return [pl.BlockSpec(memory_space=pltpu.VMEM)] * n


SMEM = pl.BlockSpec(memory_space=pltpu.SMEM)


def attention(core, queries, mine, other, d_att):
    rows, width = queries.shape
    length = mine.shape[0]
    query_like = jax.ShapeDtypeStruct(queries.shape, bf16)
    key_like = jax.ShapeDtypeStruct(mine.shape, bf16)
    return pl.pallas_call(
        attention_kernel,
        out_shape=(query_like, query_like, key_like, key_like),
        in_specs=[SMEM] + vmem_specs(4),
        out_specs=tuple(vmem_specs(4)),
        scratch_shapes=[
            pltpu.VMEM((length, E), bf16),
            pltpu.VMEM((length, E), bf16),
            pltpu.VMEM((R, length), f32),
            pltpu.VMEM((R, length), bf16),
            pltpu.VMEM((2 * E, length), f32),
        ],
        compiler_params=pltpu.CompilerParams(vmem_limit_bytes=32 * 1024 * 1024),
        cost_estimate=pl.CostEstimate(
            flops=12 * rows * length * width,
            bytes_accessed=8 * 1024 * 1024,
            transcendentals=rows * length * (width // E),
        ),
    )(core, queries, mine, other, d_att)


def prepare_kernel(place_ref, x_ref, u_ref, *refs):
    mine, other = refs[:4], refs[4:8]
    wq_ref, wo_ref, q_ref, da_ref, xt_ref = refs[8:]
    x, zh, core = place_ref[0], place_ref[1], place_ref[2]
    for side, blocks in enumerate((mine, other)):
        half = core ^ side
        for k, block in enumerate(blocks):
            for kz in range(4):
                shard = (x ^ k) * 4 + (zh ^ kz)
                wq_ref[pl.ds(pl.multiple_of(shard * 96, 32), 96), side * 256 : side * 256 + 256] = block[kz, :96, :]
                for cb in range(3):
                    wo_ref[
                        pl.ds(pl.multiple_of(shard * 32, 32), 32),
                        pl.ds(pl.multiple_of(half * 768 + cb * 256, 256), 256),
                    ] = block[kz, 96 + cb * 32 : 128 + cb * 32, :]
    q_ref[...] = dot(x_ref[...], wq_ref[:, :256], NN).astype(bf16)
    da_ref[...] = dot(u_ref[...], wo_ref[pl.ds(pl.multiple_of(core * 256, 256), 256), :], NT).astype(bf16)
    xt_ref[...] = x_ref[...].T


def prepare(place, both_inputs, both_upstream, mine, other):
    rows, width = both_inputs.shape
    return pl.pallas_call(
        prepare_kernel,
        out_shape=(
            jax.ShapeDtypeStruct((width, 512), bf16),
            jax.ShapeDtypeStruct((512, width), bf16),
            jax.ShapeDtypeStruct((rows, 256), bf16),
            jax.ShapeDtypeStruct((rows, 256), bf16),
            jax.ShapeDtypeStruct((width, rows), bf16),
        ),
        in_specs=[SMEM] + vmem_specs(10),
        out_specs=tuple(vmem_specs(5)),
        compiler_params=pltpu.CompilerParams(vmem_limit_bytes=24 * 1024 * 1024),
        cost_estimate=pl.CostEstimate(
            flops=80 * rows * width * 256, bytes_accessed=48 * 1024 * 1024, transcendentals=0
        ),
    )(place, both_inputs, both_upstream, *mine, *other)


def grads_kernel(core_ref, xt_ref, u_ref, dq_ref, att_ref, other_ref, out_ref):
    core = core_ref[0]
    rows = dq_ref.shape[0] // 2
    for g in range(4):
        q_grad = dot(xt_ref[g * 384 : (g + 1) * 384, :], dq_ref[...], NN).astype(bf16)
        out_ref[g * 4 : (g + 1) * 4, 0:96, :] = q_grad.reshape(4, 96, 256)
    mine = att_ref[...].T
    other = jnp.concatenate([other_ref[rows:, :], other_ref[:rows, :]], axis=0).T
    for cb in range(3):
        u = u_ref[:, pl.ds(pl.multiple_of(core * 768 + cb * 256, 256), 256)]
        for owner, att in ((core, mine), (1 - core, other)):
            o_grad = dot(att, u, NN).astype(bf16).reshape(8, 32, 256)
            out_ref[pl.ds(owner * 8, 8), 96 + cb * 32 : 128 + cb * 32, :] = o_grad


def grads(core, inputs_t, both_upstream, d_query, attended, other):
    return pl.pallas_call(
        grads_kernel,
        out_shape=jax.ShapeDtypeStruct((16, 192, 256), bf16),
        in_specs=[SMEM] + vmem_specs(5),
        out_specs=vmem_specs(1)[0],
        compiler_params=pltpu.CompilerParams(vmem_limit_bytes=24 * 1024 * 1024),
        cost_estimate=pl.CostEstimate(
            flops=4 * inputs_t.size * 256, bytes_accessed=6 * 1024 * 1024, transcendentals=0
        ),
    )(core, inputs_t, both_upstream, d_query, attended, other)


def unpack_kernel(core_ref, mine_ref, other_ref, q_ref, k_ref, v_ref, o_ref):
    core = core_ref[0]
    mine = mine_ref[...].astype(f32)
    other = other_ref[...].astype(f32)
    k_ref[...] = jnp.where(core == 0, mine[:96], other[:96])
    v_ref[...] = jnp.where(core == 0, other[:96], mine[:96])
    for half, part in ((core, mine), (1 - core, other)):
        for b in range(2):
            at = 96 + 192 * b
            q_ref[:, pl.ds(pl.multiple_of(half * 256 + b * E, E), E)] = part[at : at + 96]
            for cb in range(3):
                o_ref[:, pl.ds(pl.multiple_of(half * 768 + cb * 256 + b * E, E), E)] = part[
                    at + 96 + cb * 32 : at + 128 + cb * 32
                ]


def unpack(core, mine, other):
    return pl.pallas_call(
        unpack_kernel,
        out_shape=(
            jax.ShapeDtypeStruct((96, 512), f32),
            jax.ShapeDtypeStruct((96, E), f32),
            jax.ShapeDtypeStruct((96, E), f32),
            jax.ShapeDtypeStruct((32, 1536), f32),
        ),
        in_specs=[SMEM] + vmem_specs(2),
        out_specs=tuple(vmem_specs(4)),
        cost_estimate=pl.CostEstimate(flops=mine.size, bytes_accessed=mine.size * 12, transcendentals=0),
    )(core, mine, other)


def after(value, *others):
    return lax.optimization_barrier((value, others))[0]


def swap(value, axis, k, size):
    return lax.ppermute(value, axis, [(i, i ^ k) for i in range(size)])


def core_swap(value):
    return swap(value, CORE, 1, 2)


def tree_sum(values):
    values = [value.astype(f32) for value in values]
    while len(values) > 1:
        values = [a + b for a, b in zip(values[::2], values[1::2])]
    return values[0]


def shards(activations, query_weight, key_weight, value_weight, output_weight, cotangent):
    inputs = activations[0]
    upstream = cotangent[0]
    rows = inputs.shape[0]
    core = lax.axis_index(CORE)
    x = lax.axis_index(X)
    zh = lax.axis_index(ZH)
    first = core == 0

    scalar = core.astype(jnp.int32)[None]

    q_half = lax.dynamic_slice(query_weight, (0, core * 256), (96, 256))
    o_half = lax.dynamic_slice(output_weight, (0, core * 768), (32, 768))
    piece = jnp.concatenate(
        [q_half, o_half[:, :256], o_half[:, 256:512], o_half[:, 512:]], axis=0
    )
    block = jnp.stack([piece] + [swap(piece, ZH, k, 4) for k in range(1, 4)])
    blocks = [block] + [swap(block, X, k, 4) for k in range(1, 4)]

    both_inputs = jnp.concatenate([inputs, core_swap(inputs)], axis=0)
    both_upstream = jnp.concatenate([upstream, core_swap(upstream)], axis=0)

    kv_shard = jnp.where(first, key_weight, value_weight)
    w_kv = lax.all_to_all(jnp.broadcast_to(kv_shard[None], (16, 96, E)), FSDP, 0, 0).reshape(1536, E)

    kv = dot(both_inputs, w_kv, NN).astype(bf16)
    kv = jnp.where(first, kv, jnp.concatenate([kv[rows:], kv[:rows]], axis=0))
    kv = after(kv, block)
    kv_mine = lax.all_to_all(jnp.broadcast_to(kv[None], (8, 2 * rows, E)), RING, 0, 0).reshape(16 * rows, E)
    kv_other = core_swap(kv_mine)
    blocks = after(blocks, kv_mine)
    other_blocks = [core_swap(block) for block in blocks]

    w_q, w_o, queries, d_att, inputs_t = prepare(
        jnp.stack([x, zh, core]).astype(jnp.int32), both_inputs, both_upstream, blocks, other_blocks
    )
    w_all = jnp.concatenate([w_q, w_kv, core_swap(w_kv)], axis=1)

    attended, d_query, kept, sent = attention(scalar, queries, kv_mine, kv_other, d_att)

    attended_other = core_swap(attended)
    terms = grads(scalar, inputs_t, both_upstream, d_query, attended, attended_other)
    x_terms = [lax.dynamic_slice(terms, ((x ^ k) * 4, 0, 0), (4, 192, 256)) for k in range(4)]

    d_kv = (kept.astype(f32) + core_swap(sent).astype(f32)).astype(bf16).reshape(8, 2 * rows, E)
    d_kv = lax.all_to_all(after(d_kv, x_terms), RING, 0, 0)
    d_mine = jnp.sum(d_kv.astype(f32), axis=0).astype(bf16)

    x_got = after([x_terms[0]] + [swap(x_terms[k], X, k, 4) for k in range(1, 4)], d_kv)
    terms = tree_sum(x_got).astype(bf16)
    z_terms = [lax.dynamic_index_in_dim(terms, zh ^ k, 0, keepdims=False) for k in range(4)]

    d_own = lax.dynamic_slice(d_mine, (core * rows, 0), (rows, E))
    d_next = lax.dynamic_slice(d_mine, ((1 - core) * rows, 0), (rows, E))
    kv_grad = dot(inputs_t, jnp.concatenate([d_own, d_next], axis=0), NN).astype(bf16)
    kv_terms = lax.all_to_all(after(kv_grad.reshape(16, 96, E), z_terms), FSDP, 0, 0)
    kv_sum = jnp.sum(kv_terms.astype(f32), axis=0).astype(bf16)
    z_got = after([z_terms[0]] + [swap(z_terms[k], ZH, k, 4) for k in range(1, 4)], kv_terms)
    qo_sum = tree_sum(z_got).astype(bf16)

    share = jnp.concatenate([kv_sum, qo_sum[:, :E], qo_sum[:, E:]], axis=0)
    terms = lax.all_to_all(jnp.broadcast_to(share[None], (8, 480, E)), RING, 0, 0)
    final = lax.optimization_barrier(jnp.sum(terms.astype(f32), axis=0).astype(bf16))
    query_grad, key_grad, value_grad, output_grad = unpack(scalar, final, core_swap(final))

    w_o_mine = lax.dynamic_slice(w_o, (core * 256, 0), (256, 1536))
    w_o_other = lax.dynamic_slice(w_o, ((1 - core) * 256, 0), (256, 1536))
    layer_out = dot(
        jnp.concatenate([attended[:rows], attended_other[rows:]], axis=1),
        jnp.concatenate([w_o_mine, w_o_other], axis=0),
        NN,
    ).astype(bf16)
    d_all = jnp.concatenate([d_query[:rows], core_swap(d_query[rows:]), d_own, core_swap(d_next)], axis=1)
    input_grad = dot(d_all, w_all, NT).astype(bf16)
    return (layer_out[None], input_grad[None], query_grad, key_grad, value_grad, output_grad)


def solution(mesh):
    split = Mesh(mesh.devices.reshape(2, 4, 2, 4, 4), (ZL, Y, CORE, X, ZH))
    seq = (ZL, Y, CORE)
    return jax.shard_map(
        shards,
        mesh=split,
        in_specs=(
            P(FSDP, seq, None),
            P(FSDP, None),
            P(FSDP, None),
            P(FSDP, None),
            P(FSDP, None),
            P(FSDP, seq, None),
        ),
        out_specs=(
            P(FSDP, seq, None),
            P(FSDP, seq, None),
            P(FSDP, None),
            P(FSDP, None),
            P(FSDP, None),
            P(FSDP, None),
        ),
        check_vma=False,
    )
```

```python
import math

import jax
import jax.numpy as jnp
from jax import lax
from jax.experimental import pallas as pl
from jax.experimental.pallas import tpu as pltpu
from jax.sharding import Mesh, PartitionSpec as P

f32 = jnp.float32
bf16 = jnp.bfloat16

NT = (((1,), (1,)), ((), ()))
NN = (((1,), (0,)), ((), ()))
TN = (((0,), (0,)), ((), ()))

E = 128
R = 256
C = 1024

ZL, Y, CORE, X, ZH = "zl", "y", "core", "x", "zh"
FSDP = (X, ZH)
RING = (ZL, Y)


def dot(a, b, dims):
    return lax.dot_general(a, b, dims, preferred_element_type=f32)


def start(pairs, sems):
    copies = [pltpu.make_async_copy(src, dst, sems.at[n]) for n, (src, dst) in enumerate(pairs)]
    for copy in copies:
        copy.start()
    return copies


def fetch(pairs, sems):
    for copy in start(pairs, sems):
        copy.wait()


def attention_kernel(
    core_ref, q_ref, mine_ref, other_ref, do_ref,
    att_ref, dq_ref, kept_ref, sent_ref,
    k_ref, v_ref, s_ref, e_ref, acc_ref, sems,
):
    length = k_ref.shape[0]
    rows, width = q_ref.shape
    scale = 1.0 / math.sqrt(E)
    scale2 = scale * math.log2(math.e)
    first = core_ref[0] == 0

    @pl.when(first)
    def _():
        fetch([(mine_ref, k_ref), (other_ref, v_ref)], sems)

    @pl.when(jnp.logical_not(first))
    def _():
        fetch([(other_ref, k_ref), (mine_ref, v_ref)], sems)

    blocks = [(r, h) for h in range(width // E) for r in range(rows // R)]
    for n, (r, h) in enumerate(blocks):
        at = (slice(r * R, (r + 1) * R), slice(h * E, (h + 1) * E))
        q = q_ref[at]
        top = jnp.full((R, E), -jnp.inf, f32)
        for i in range(length // C):
            part = slice(i * C, (i + 1) * C)
            s = dot(q, k_ref[part, :], NT)
            s_ref[:, part] = s
            for t in range(C // E):
                top = jnp.maximum(top, s[:, t * E : (t + 1) * E])
        top = jnp.max(top, axis=1, keepdims=True) * scale2
        total = jnp.zeros((R, E), f32)
        out = jnp.zeros((R, E), f32)
        for i in range(length // C):
            part = slice(i * C, (i + 1) * C)
            e = jnp.exp2(s_ref[:, part] * scale2 - top)
            for t in range(C // E):
                total = total + e[:, t * E : (t + 1) * E]
            eb = e.astype(bf16)
            e_ref[:, part] = eb
            out = out + dot(eb, v_ref[part, :], NN)
        inverse = 1.0 / jnp.sum(total, axis=1, keepdims=True)
        out = out * inverse
        att_ref[at] = out.astype(bf16)
        do = (do_ref[at].astype(f32) * inverse).astype(bf16)
        delta = jnp.sum(do.astype(f32) * out, axis=1, keepdims=True)
        dq = jnp.zeros((R, E), f32)
        q_t = q.T
        do_t = do.T
        for i in range(length // C):
            part = slice(i * C, (i + 1) * C)
            dp = dot(do, v_ref[part, :], NT)
            eb = e_ref[:, part]
            ds = (eb.astype(f32) * (dp - delta)).astype(bf16)
            dk = dot(q_t, ds, NN)
            dv = dot(do_t, eb, NN)
            if n == 0:
                acc_ref[0:E, part] = dk
                acc_ref[E : 2 * E, part] = dv
            elif n < len(blocks) - 1:
                acc_ref[0:E, part] += dk
                acc_ref[E : 2 * E, part] += dv
            else:
                dk = (acc_ref[0:E, part] + dk) * scale
                dv = acc_ref[E : 2 * E, part] + dv
                kept_ref[part, :] = jnp.where(first, dk, dv).T.astype(bf16)
                sent_ref[part, :] = jnp.where(first, dv, dk).T.astype(bf16)
            dq = dq + dot(ds, k_ref[part, :], NN)
        dq_ref[at] = (dq * scale).astype(bf16)


def vmem_specs(n):
    return [pl.BlockSpec(memory_space=pltpu.VMEM)] * n


def any_specs(n):
    return [pl.BlockSpec(memory_space=pl.ANY)] * n


SMEM = pl.BlockSpec(memory_space=pltpu.SMEM)


def attention(core, queries, mine, other, d_att):
    rows, width = queries.shape
    length = mine.shape[0]
    query_like = jax.ShapeDtypeStruct(queries.shape, bf16)
    key_like = jax.ShapeDtypeStruct(mine.shape, bf16)
    return pl.pallas_call(
        attention_kernel,
        out_shape=(query_like, query_like, key_like, key_like),
        in_specs=[SMEM] + vmem_specs(1) + any_specs(2) + vmem_specs(1),
        out_specs=tuple(vmem_specs(4)),
        scratch_shapes=[
            pltpu.VMEM((length, E), bf16),
            pltpu.VMEM((length, E), bf16),
            pltpu.VMEM((R, length), f32),
            pltpu.VMEM((R, length), bf16),
            pltpu.VMEM((2 * E, length), f32),
            pltpu.SemaphoreType.DMA((2,)),
        ],
        compiler_params=pltpu.CompilerParams(vmem_limit_bytes=58 * 1024 * 1024),
        cost_estimate=pl.CostEstimate(
            flops=12 * rows * length * width,
            bytes_accessed=8 * 1024 * 1024,
            transcendentals=rows * length * (width // E),
        ),
    )(core, queries, mine, other, d_att)


def prepare_kernel(place_ref, x0_ref, x1_ref, u0_ref, u1_ref, *refs):
    arrived = refs[:8]
    wq_ref, wo_ref, q_ref, da_ref, xt_ref, x_ref, u_ref, blocks, sems = refs[8:]
    x, zh, core = place_ref[0], place_ref[1], place_ref[2]
    copies = start(
        [(ref, blocks.at[n]) for n, ref in enumerate(arrived)]
        + [(x0_ref, x_ref.at[:R]), (x1_ref, x_ref.at[R:]), (u0_ref, u_ref.at[:R]), (u1_ref, u_ref.at[R:])],
        sems,
    )
    for n in range(8):
        copies[n].wait()
        side, k = n // 4, n % 4
        half = core ^ side
        for kz in range(4):
            shard = (x ^ k) * 4 + (zh ^ kz)
            wq_ref[pl.ds(pl.multiple_of(shard * 96, 32), 96), side * 256 : side * 256 + 256] = blocks[n, kz, :96, :]
            for cb in range(3):
                wo_ref[
                    pl.ds(pl.multiple_of(shard * 32, 32), 32),
                    pl.ds(pl.multiple_of(half * 768 + cb * 256, 256), 256),
                ] = blocks[n, kz, 96 + cb * 32 : 128 + cb * 32, :]
    for n in range(8, 12):
        copies[n].wait()
    q_ref[...] = dot(x_ref[...], wq_ref[:, :256], NN).astype(bf16)
    w_o = wo_ref[pl.ds(pl.multiple_of(core * 256, 256), 256), :]
    da_ref[...] = dot(u_ref[...], w_o, NT).astype(bf16)
    xt_ref[...] = x_ref[...].T


def prepare(place, inputs, inputs_next, upstream, upstream_next, mine, other):
    rows, width = 2 * inputs.shape[0], inputs.shape[1]
    return pl.pallas_call(
        prepare_kernel,
        out_shape=(
            jax.ShapeDtypeStruct((width, 512), bf16),
            jax.ShapeDtypeStruct((512, width), bf16),
            jax.ShapeDtypeStruct((rows, 256), bf16),
            jax.ShapeDtypeStruct((rows, 256), bf16),
            jax.ShapeDtypeStruct((width, rows), bf16),
        ),
        in_specs=[SMEM] + any_specs(12),
        out_specs=tuple(vmem_specs(5)),
        scratch_shapes=[
            pltpu.VMEM((rows, width), bf16),
            pltpu.VMEM((rows, width), bf16),
            pltpu.VMEM((8, 4, 192, 256), bf16),
            pltpu.SemaphoreType.DMA((12,)),
        ],
        compiler_params=pltpu.CompilerParams(vmem_limit_bytes=58 * 1024 * 1024),
        cost_estimate=pl.CostEstimate(
            flops=80 * rows * width * 256, bytes_accessed=48 * 1024 * 1024, transcendentals=0
        ),
    )(place, inputs, inputs_next, upstream, upstream_next, *mine, *other)


def pack_kernel(core_ref, q_ref, k_ref, v_ref, o_ref, out_ref):
    core = core_ref[0]
    kv = jnp.where(core == 0, k_ref[...].astype(f32), v_ref[...].astype(f32)).astype(bf16)
    out_ref[:48, :E] = kv[:48]
    out_ref[:48, E:] = kv[48:]
    out_ref[48:144, :] = q_ref[:, pl.ds(pl.multiple_of(core * 256, 256), 256)]
    for cb in range(3):
        out_ref[144 + cb * 32 : 176 + cb * 32, :] = o_ref[
            :, pl.ds(pl.multiple_of(core * 768 + cb * 256, 256), 256)
        ]


def pack(core, *weights):
    return pl.pallas_call(
        pack_kernel,
        out_shape=jax.ShapeDtypeStruct((240, 256), bf16),
        in_specs=[SMEM] + vmem_specs(4),
        out_specs=vmem_specs(1)[0],
    )(core, *weights)


def kv_kernel(place_ref, x0_ref, x1_ref, w0, w1, w2, w3, w_ref, out_ref, x_ref, blocks, sems):
    x, zh, core = place_ref[0], place_ref[1], place_ref[2]
    copies = start(
        [(ref, blocks.at[k]) for k, ref in enumerate((w0, w1, w2, w3))]
        + [(x0_ref, x_ref.at[:R]), (x1_ref, x_ref.at[R:])],
        sems,
    )
    for k in range(4):
        copies[k].wait()
        for kz in range(4):
            first_row = ((x ^ k) * 4 + (zh ^ kz)) * 96
            w_ref[pl.ds(pl.multiple_of(first_row, 32), 96), :] = blocks[k, kz]
    copies[4].wait()
    copies[5].wait()
    for n, owner in enumerate((core, 1 - core)):
        kv = dot(x_ref[n * R : (n + 1) * R, :], w_ref[...], NN).astype(bf16)
        for chip in range(8):
            out_ref[chip, pl.ds(pl.multiple_of(owner * R, R), R), :] = kv


def keys_or_values(place, inputs, inputs_next, blocks):
    rows, width = inputs.shape
    return pl.pallas_call(
        kv_kernel,
        out_shape=(
            jax.ShapeDtypeStruct((width, E), bf16),
            jax.ShapeDtypeStruct((8, 2 * rows, E), bf16),
        ),
        in_specs=[SMEM] + any_specs(6),
        out_specs=tuple(vmem_specs(2)),
        scratch_shapes=[
            pltpu.VMEM((2 * rows, width), bf16),
            pltpu.VMEM((4, 4, 96, E), bf16),
            pltpu.SemaphoreType.DMA((6,)),
        ],
        compiler_params=pltpu.CompilerParams(vmem_limit_bytes=58 * 1024 * 1024),
        cost_estimate=pl.CostEstimate(
            flops=4 * rows * width * E, bytes_accessed=4 * 1024 * 1024, transcendentals=0
        ),
    )(place, inputs, inputs_next, *blocks)


def grads_kernel(core_ref, xt_hbm, u0_hbm, u1_hbm, dq_hbm, att_hbm, other_hbm, out_ref, xt_ref, u_ref, small, sems):
    core = core_ref[0]
    half = pl.ds(pl.multiple_of(core * 768, 256), 768)
    copies = start(
        [
            (att_hbm, small.at[0]),
            (other_hbm.at[:R], small.at[1, R:]),
            (other_hbm.at[R:], small.at[1, :R]),
            (u0_hbm.at[:, half], u_ref.at[:R]),
            (u1_hbm.at[:, half], u_ref.at[R:]),
            (dq_hbm, small.at[2]),
            (xt_hbm, xt_ref),
        ],
        sems,
    )
    for n in range(5):
        copies[n].wait()
    for n, owner in enumerate((core, 1 - core)):
        att = small[n].T
        for cb in range(3):
            o_grad = dot(att, u_ref[:, cb * 256 : (cb + 1) * 256], NN).astype(bf16).reshape(8, 32, 256)
            out_ref[pl.ds(owner * 8, 8), 96 + cb * 32 : 128 + cb * 32, :] = o_grad
    copies[5].wait()
    copies[6].wait()
    for g in range(4):
        q_grad = dot(xt_ref[g * 384 : (g + 1) * 384, :], small[2], NN).astype(bf16)
        out_ref[g * 4 : (g + 1) * 4, 0:96, :] = q_grad.reshape(4, 96, 256)


def grads(core, inputs_t, upstream, upstream_next, d_query, attended, other):
    return pl.pallas_call(
        grads_kernel,
        out_shape=jax.ShapeDtypeStruct((16, 192, 256), bf16),
        in_specs=[SMEM] + any_specs(6),
        out_specs=vmem_specs(1)[0],
        scratch_shapes=[
            pltpu.VMEM(inputs_t.shape, bf16),
            pltpu.VMEM((2 * R, 768), bf16),
            pltpu.VMEM((3, 2 * R, 256), bf16),
            pltpu.SemaphoreType.DMA((7,)),
        ],
        compiler_params=pltpu.CompilerParams(vmem_limit_bytes=58 * 1024 * 1024),
        cost_estimate=pl.CostEstimate(
            flops=4 * inputs_t.size * 256, bytes_accessed=6 * 1024 * 1024, transcendentals=0
        ),
    )(core, inputs_t, upstream, upstream_next, d_query, attended, other)


def unpack_kernel(core_ref, mine_ref, other_ref, q_ref, k_ref, v_ref, o_ref):
    core = core_ref[0]
    mine = mine_ref[...].astype(f32)
    other = other_ref[...].astype(f32)
    k_ref[...] = jnp.where(core == 0, mine[:96], other[:96])
    v_ref[...] = jnp.where(core == 0, other[:96], mine[:96])
    for half, part in ((core, mine), (1 - core, other)):
        for b in range(2):
            at = 96 + 192 * b
            q_ref[:, pl.ds(pl.multiple_of(half * 256 + b * E, E), E)] = part[at : at + 96]
            for cb in range(3):
                o_ref[:, pl.ds(pl.multiple_of(half * 768 + cb * 256 + b * E, E), E)] = part[
                    at + 96 + cb * 32 : at + 128 + cb * 32
                ]


def unpack(core, mine, other):
    return pl.pallas_call(
        unpack_kernel,
        out_shape=(
            jax.ShapeDtypeStruct((96, 512), f32),
            jax.ShapeDtypeStruct((96, E), f32),
            jax.ShapeDtypeStruct((96, E), f32),
            jax.ShapeDtypeStruct((32, 1536), f32),
        ),
        in_specs=[SMEM] + vmem_specs(2),
        out_specs=tuple(vmem_specs(4)),
        cost_estimate=pl.CostEstimate(flops=mine.size, bytes_accessed=mine.size * 12, transcendentals=0),
    )(core, mine, other)


def after(value, *others):
    return lax.optimization_barrier((value, others))[0]


def swap(value, axis, k, size):
    return lax.ppermute(value, axis, [(i, i ^ k) for i in range(size)])


def core_swap(value):
    return swap(value, CORE, 1, 2)


def tree_sum(values):
    values = [value.astype(f32) for value in values]
    while len(values) > 1:
        values = [a + b for a, b in zip(values[::2], values[1::2])]
    return values[0]


def shards(activations, query_weight, key_weight, value_weight, output_weight, cotangent):
    inputs = activations[0]
    upstream = cotangent[0]
    rows = inputs.shape[0]
    core = lax.axis_index(CORE)
    x = lax.axis_index(X)
    zh = lax.axis_index(ZH)

    scalar = core.astype(jnp.int32)[None]

    place = jnp.stack([x, zh, core]).astype(jnp.int32)

    piece = pack(scalar, query_weight, key_weight, value_weight, output_weight)
    inputs_next = core_swap(inputs)
    upstream_next = core_swap(upstream)
    pieces = [piece] + [swap(piece, ZH, k, 4) for k in range(1, 4)]
    kv_block = jnp.stack([jnp.concatenate([p[:48, :E], p[:48, E:]], axis=0) for p in pieces])
    block = jnp.stack([p[48:] for p in pieces])
    block, kv_block = after((block, kv_block), inputs_next, upstream_next)
    kv_blocks = [kv_block] + [swap(kv_block, X, k, 4) for k in range(1, 4)]
    blocks = [block] + [swap(block, X, k, 4) for k in range(1, 4)]

    w_kv, kv = keys_or_values(place, inputs, inputs_next, kv_blocks)
    kv = after(kv, blocks[1])
    kv_mine = lax.all_to_all(kv, RING, 0, 0).reshape(16 * rows, E)
    kv_other = core_swap(kv_mine)

    other_blocks = [core_swap(block) for block in blocks]
    w_q, w_o, queries, d_att, inputs_t = prepare(
        place, inputs, inputs_next, upstream, upstream_next, blocks, other_blocks
    )
    w_all = jnp.concatenate([w_q, w_kv, core_swap(w_kv)], axis=1)

    attended, d_query, kept, sent = attention(scalar, queries, kv_mine, kv_other, d_att)

    attended_other = core_swap(attended)
    terms = grads(scalar, inputs_t, upstream, upstream_next, d_query, attended, attended_other)
    x_terms = [lax.dynamic_slice(terms, ((x ^ k) * 4, 0, 0), (4, 192, 256)) for k in range(4)]

    d_kv = (kept.astype(f32) + core_swap(sent).astype(f32)).astype(bf16).reshape(8, 2 * rows, E)
    d_kv = lax.all_to_all(after(d_kv, x_terms), RING, 0, 0)
    d_mine = jnp.sum(d_kv.astype(f32), axis=0).astype(bf16)

    d_own = lax.dynamic_slice(d_mine, (core * rows, 0), (rows, E))
    d_next = lax.dynamic_slice(d_mine, ((1 - core) * rows, 0), (rows, E))
    kv_grad = dot(inputs_t, jnp.concatenate([d_own, d_next], axis=0), NN).astype(bf16)
    kv_terms = lax.all_to_all(kv_grad.reshape(16, 96, E), FSDP, 0, 0)
    x_got = after([x_terms[0]] + [swap(x_terms[k], X, k, 4) for k in range(1, 4)], kv_grad)
    terms = tree_sum(x_got).astype(bf16)
    z_terms = [lax.dynamic_index_in_dim(terms, zh ^ k, 0, keepdims=False) for k in range(4)]
    kv_sum = jnp.sum(kv_terms.astype(f32), axis=0).astype(bf16)
    z_got = after([z_terms[0]] + [swap(z_terms[k], ZH, k, 4) for k in range(1, 4)], kv_terms)
    qo_sum = tree_sum(z_got).astype(bf16)

    w_o_mine = lax.dynamic_slice(w_o, (core * 256, 0), (256, 1536))
    w_o_other = lax.dynamic_slice(w_o, ((1 - core) * 256, 0), (256, 1536))
    layer_out = dot(
        jnp.concatenate([attended[:rows], attended_other[rows:]], axis=1),
        jnp.concatenate([w_o_mine, w_o_other], axis=0),
        NN,
    ).astype(bf16)
    d_all = jnp.concatenate([d_query[:rows], core_swap(d_query[rows:]), d_own, core_swap(d_next)], axis=1)
    input_grad = dot(d_all, w_all, NT).astype(bf16)
    share = jnp.concatenate([kv_sum, qo_sum[:, :E], qo_sum[:, E:]], axis=0)
    terms = after(lax.all_to_all(jnp.broadcast_to(share[None], (8, 480, E)), RING, 0, 0), layer_out, input_grad)
    final = lax.optimization_barrier(jnp.sum(terms.astype(f32), axis=0).astype(bf16))
    query_grad, key_grad, value_grad, output_grad = unpack(scalar, final, core_swap(final))

    return (layer_out[None], input_grad[None], query_grad, key_grad, value_grad, output_grad)


def solution(mesh):
    split = Mesh(mesh.devices.reshape(2, 4, 2, 4, 4), (ZL, Y, CORE, X, ZH))
    seq = (ZL, Y, CORE)
    return jax.shard_map(
        shards,
        mesh=split,
        in_specs=(
            P(FSDP, seq, None),
            P(FSDP, None),
            P(FSDP, None),
            P(FSDP, None),
            P(FSDP, None),
            P(FSDP, seq, None),
        ),
        out_specs=(
            P(FSDP, seq, None),
            P(FSDP, seq, None),
            P(FSDP, None),
            P(FSDP, None),
            P(FSDP, None),
            P(FSDP, None),
        ),
        check_vma=False,
    )
```

```python
import math

import jax
import jax.numpy as jnp
from jax import lax
from jax.experimental import pallas as pl
from jax.experimental.pallas import tpu as pltpu
from jax.sharding import Mesh, PartitionSpec as P

f32 = jnp.float32
bf16 = jnp.bfloat16

NT = (((1,), (1,)), ((), ()))
NN = (((1,), (0,)), ((), ()))
TN = (((0,), (0,)), ((), ()))

E = 128
R = 256
C = 1024

ZL, Y, CORE, X, ZH = "zl", "y", "core", "x", "zh"
FSDP = (X, ZH)
RING = (ZL, Y)


def dot(a, b, dims):
    return lax.dot_general(a, b, dims, preferred_element_type=f32)


def start(pairs, sems):
    copies = [pltpu.make_async_copy(src, dst, sems.at[n]) for n, (src, dst) in enumerate(pairs)]
    for copy in copies:
        copy.start()
    return copies


def fetch(pairs, sems):
    for copy in start(pairs, sems):
        copy.wait()


def attention_kernel(
    core_ref, q_ref, mine_ref, other_ref, do_ref,
    att_ref, dq_ref, kept_ref, sent_ref,
    k_ref, v_ref, s_ref, e_ref, acc_ref, sems,
):
    length = k_ref.shape[0]
    rows, width = q_ref.shape
    scale = 1.0 / math.sqrt(E)
    scale2 = scale * math.log2(math.e)
    first = core_ref[0] == 0

    @pl.when(first)
    def _():
        fetch([(mine_ref, k_ref), (other_ref, v_ref)], sems)

    @pl.when(jnp.logical_not(first))
    def _():
        fetch([(other_ref, k_ref), (mine_ref, v_ref)], sems)

    blocks = [(r, h) for h in range(width // E) for r in range(rows // R)]
    for n, (r, h) in enumerate(blocks):
        at = (slice(r * R, (r + 1) * R), slice(h * E, (h + 1) * E))
        q = q_ref[at]
        top = jnp.full((R, E), -jnp.inf, f32)
        for i in range(length // C):
            part = slice(i * C, (i + 1) * C)
            s = dot(q, k_ref[part, :], NT)
            s_ref[:, part] = s
            for t in range(C // E):
                top = jnp.maximum(top, s[:, t * E : (t + 1) * E])
        top = jnp.max(top, axis=1, keepdims=True) * scale2
        total = jnp.zeros((R, E), f32)
        out = jnp.zeros((R, E), f32)
        for i in range(length // C):
            part = slice(i * C, (i + 1) * C)
            e = jnp.exp2(s_ref[:, part] * scale2 - top)
            for t in range(C // E):
                total = total + e[:, t * E : (t + 1) * E]
            eb = e.astype(bf16)
            e_ref[:, part] = eb
            out = out + dot(eb, v_ref[part, :], NN)
        inverse = 1.0 / jnp.sum(total, axis=1, keepdims=True)
        out = out * inverse
        att_ref[at] = out.astype(bf16)
        do = (do_ref[at].astype(f32) * inverse).astype(bf16)
        delta = jnp.sum(do.astype(f32) * out, axis=1, keepdims=True)
        dq = jnp.zeros((R, E), f32)
        q_t = q.T
        do_t = do.T
        for i in range(length // C):
            part = slice(i * C, (i + 1) * C)
            dp = dot(do, v_ref[part, :], NT)
            eb = e_ref[:, part]
            ds = (eb.astype(f32) * (dp - delta)).astype(bf16)
            dk = dot(q_t, ds, NN)
            dv = dot(do_t, eb, NN)
            if n == 0:
                acc_ref[0:E, part] = dk
                acc_ref[E : 2 * E, part] = dv
            elif n < len(blocks) - 1:
                acc_ref[0:E, part] += dk
                acc_ref[E : 2 * E, part] += dv
            else:
                dk = (acc_ref[0:E, part] + dk) * scale
                dv = acc_ref[E : 2 * E, part] + dv
                kept_ref[part, :] = jnp.where(first, dk, dv).T.astype(bf16)
                sent_ref[part, :] = jnp.where(first, dv, dk).T.astype(bf16)
            dq = dq + dot(ds, k_ref[part, :], NN)
        dq_ref[at] = (dq * scale).astype(bf16)


def vmem_specs(n):
    return [pl.BlockSpec(memory_space=pltpu.VMEM)] * n


def any_specs(n):
    return [pl.BlockSpec(memory_space=pl.ANY)] * n


SMEM = pl.BlockSpec(memory_space=pltpu.SMEM)


def attention(core, queries, mine, other, d_att):
    rows, width = queries.shape
    length = mine.shape[0]
    query_like = jax.ShapeDtypeStruct(queries.shape, bf16)
    key_like = jax.ShapeDtypeStruct(mine.shape, bf16)
    return pl.pallas_call(
        attention_kernel,
        out_shape=(query_like, query_like, key_like, key_like),
        in_specs=[SMEM] + vmem_specs(1) + any_specs(2) + vmem_specs(1),
        out_specs=tuple(vmem_specs(4)),
        scratch_shapes=[
            pltpu.VMEM((length, E), bf16),
            pltpu.VMEM((length, E), bf16),
            pltpu.VMEM((R, length), f32),
            pltpu.VMEM((R, length), bf16),
            pltpu.VMEM((2 * E, length), f32),
            pltpu.SemaphoreType.DMA((2,)),
        ],
        compiler_params=pltpu.CompilerParams(vmem_limit_bytes=58 * 1024 * 1024),
        cost_estimate=pl.CostEstimate(
            flops=12 * rows * length * width,
            bytes_accessed=8 * 1024 * 1024,
            transcendentals=rows * length * (width // E),
        ),
    )(core, queries, mine, other, d_att)


def prepare_kernel(place_ref, x0_ref, x1_ref, u0_ref, u1_ref, *refs):
    arrived = refs[:8]
    wq_ref, wo_ref, q_ref, da_ref, xt_ref, x_ref, u_ref, blocks, sems = refs[8:]
    x, zh, core, y = place_ref[0], place_ref[1], place_ref[2], place_ref[3]
    copies = start(
        [
            (ref.at[ky], blocks.at[n, :, pl.ds(pl.multiple_of((y ^ ky) * 48, 16), 48), :])
            for n, ref in enumerate(arrived)
            for ky in range(4)
        ]
        + [(x0_ref, x_ref.at[:R]), (x1_ref, x_ref.at[R:]), (u0_ref, u_ref.at[:R]), (u1_ref, u_ref.at[R:])],
        sems,
    )
    for n in range(8):
        for ky in range(4):
            copies[n * 4 + ky].wait()
        side, k = n // 4, n % 4
        half = core ^ side
        for kz in range(4):
            shard = (x ^ k) * 4 + (zh ^ kz)
            wq_ref[pl.ds(pl.multiple_of(shard * 96, 32), 96), side * 256 : side * 256 + 256] = blocks[n, kz, :96, :]
            for cb in range(3):
                wo_ref[
                    pl.ds(pl.multiple_of(shard * 32, 32), 32),
                    pl.ds(pl.multiple_of(half * 768 + cb * 256, 256), 256),
                ] = blocks[n, kz, 96 + cb * 32 : 128 + cb * 32, :]
    for n in range(32, 36):
        copies[n].wait()
    q_ref[...] = dot(x_ref[...], wq_ref[:, :256], NN).astype(bf16)
    w_o = wo_ref[pl.ds(pl.multiple_of(core * 256, 256), 256), :]
    da_ref[...] = dot(u_ref[...], w_o, NT).astype(bf16)
    xt_ref[...] = x_ref[...].T


def prepare(place, inputs, inputs_next, upstream, upstream_next, mine, other):
    rows, width = 2 * inputs.shape[0], inputs.shape[1]
    return pl.pallas_call(
        prepare_kernel,
        out_shape=(
            jax.ShapeDtypeStruct((width, 512), bf16),
            jax.ShapeDtypeStruct((512, width), bf16),
            jax.ShapeDtypeStruct((rows, 256), bf16),
            jax.ShapeDtypeStruct((rows, 256), bf16),
            jax.ShapeDtypeStruct((width, rows), bf16),
        ),
        in_specs=[SMEM] + any_specs(12),
        out_specs=tuple(vmem_specs(5)),
        scratch_shapes=[
            pltpu.VMEM((rows, width), bf16),
            pltpu.VMEM((rows, width), bf16),
            pltpu.VMEM((8, 4, 192, 256), bf16),
            pltpu.SemaphoreType.DMA((36,)),
        ],
        compiler_params=pltpu.CompilerParams(vmem_limit_bytes=58 * 1024 * 1024),
        cost_estimate=pl.CostEstimate(
            flops=80 * rows * width * 256, bytes_accessed=48 * 1024 * 1024, transcendentals=0
        ),
    )(place, inputs, inputs_next, upstream, upstream_next, *mine, *other)


def pack_kernel(place_ref, q_ref, k_ref, v_ref, o_ref, out_ref, rows_ref):
    core, y = place_ref[2], place_ref[3]
    kv = jnp.where(core == 0, k_ref[...].astype(f32), v_ref[...].astype(f32)).astype(bf16)
    out_ref[:48, :E] = kv[:48]
    out_ref[:48, E:] = kv[48:]
    rows_ref[:96, :] = q_ref[:, pl.ds(pl.multiple_of(core * 256, 256), 256)]
    for cb in range(3):
        rows_ref[96 + cb * 32 : 128 + cb * 32, :] = o_ref[
            :, pl.ds(pl.multiple_of(core * 768 + cb * 256, 256), 256)
        ]
    out_ref[48:, :] = rows_ref[pl.ds(pl.multiple_of(y * 48, 16), 48), :]


def pack(place, *weights):
    return pl.pallas_call(
        pack_kernel,
        out_shape=jax.ShapeDtypeStruct((96, 256), bf16),
        in_specs=[SMEM] + vmem_specs(4),
        out_specs=vmem_specs(1)[0],
        scratch_shapes=[pltpu.VMEM((192, 256), bf16)],
    )(place, *weights)


def kv_kernel(place_ref, x0_ref, x1_ref, w0, w1, w2, w3, w_ref, out_ref, x_ref, blocks, sems):
    x, zh, core = place_ref[0], place_ref[1], place_ref[2]
    copies = start(
        [(ref, blocks.at[k]) for k, ref in enumerate((w0, w1, w2, w3))]
        + [(x0_ref, x_ref.at[:R]), (x1_ref, x_ref.at[R:])],
        sems,
    )
    for k in range(4):
        copies[k].wait()
        for kz in range(4):
            first_row = ((x ^ k) * 4 + (zh ^ kz)) * 96
            w_ref[pl.ds(pl.multiple_of(first_row, 32), 96), :] = blocks[k, kz]
    copies[4].wait()
    copies[5].wait()
    for n, owner in enumerate((core, 1 - core)):
        kv = dot(x_ref[n * R : (n + 1) * R, :], w_ref[...], NN).astype(bf16)
        for chip in range(8):
            out_ref[chip, pl.ds(pl.multiple_of(owner * R, R), R), :] = kv


def keys_or_values(place, inputs, inputs_next, blocks):
    rows, width = inputs.shape
    return pl.pallas_call(
        kv_kernel,
        out_shape=(
            jax.ShapeDtypeStruct((width, E), bf16),
            jax.ShapeDtypeStruct((8, 2 * rows, E), bf16),
        ),
        in_specs=[SMEM] + any_specs(6),
        out_specs=tuple(vmem_specs(2)),
        scratch_shapes=[
            pltpu.VMEM((2 * rows, width), bf16),
            pltpu.VMEM((4, 4, 96, E), bf16),
            pltpu.SemaphoreType.DMA((6,)),
        ],
        compiler_params=pltpu.CompilerParams(vmem_limit_bytes=58 * 1024 * 1024),
        cost_estimate=pl.CostEstimate(
            flops=4 * rows * width * E, bytes_accessed=4 * 1024 * 1024, transcendentals=0
        ),
    )(place, inputs, inputs_next, *blocks)


def grads_kernel(core_ref, xt_hbm, u0_hbm, u1_hbm, dq_hbm, att_hbm, other_hbm, out_ref, xt_ref, u_ref, small, sems):
    core = core_ref[0]
    half = pl.ds(pl.multiple_of(core * 768, 256), 768)
    copies = start(
        [
            (att_hbm, small.at[0]),
            (other_hbm.at[:R], small.at[1, R:]),
            (other_hbm.at[R:], small.at[1, :R]),
            (u0_hbm.at[:, half], u_ref.at[:R]),
            (u1_hbm.at[:, half], u_ref.at[R:]),
            (dq_hbm, small.at[2]),
            (xt_hbm, xt_ref),
        ],
        sems,
    )
    for n in range(5):
        copies[n].wait()
    for n, owner in enumerate((core, 1 - core)):
        att = small[n].T
        for cb in range(3):
            o_grad = dot(att, u_ref[:, cb * 256 : (cb + 1) * 256], NN).astype(bf16).reshape(8, 32, 256)
            out_ref[pl.ds(owner * 8, 8), 96 + cb * 32 : 128 + cb * 32, :] = o_grad
    copies[5].wait()
    copies[6].wait()
    for g in range(4):
        q_grad = dot(xt_ref[g * 384 : (g + 1) * 384, :], small[2], NN).astype(bf16)
        out_ref[g * 4 : (g + 1) * 4, 0:96, :] = q_grad.reshape(4, 96, 256)


def grads(core, inputs_t, upstream, upstream_next, d_query, attended, other):
    return pl.pallas_call(
        grads_kernel,
        out_shape=jax.ShapeDtypeStruct((16, 192, 256), bf16),
        in_specs=[SMEM] + any_specs(6),
        out_specs=vmem_specs(1)[0],
        scratch_shapes=[
            pltpu.VMEM(inputs_t.shape, bf16),
            pltpu.VMEM((2 * R, 768), bf16),
            pltpu.VMEM((3, 2 * R, 256), bf16),
            pltpu.SemaphoreType.DMA((7,)),
        ],
        compiler_params=pltpu.CompilerParams(vmem_limit_bytes=58 * 1024 * 1024),
        cost_estimate=pl.CostEstimate(
            flops=4 * inputs_t.size * 256, bytes_accessed=6 * 1024 * 1024, transcendentals=0
        ),
    )(core, inputs_t, upstream, upstream_next, d_query, attended, other)


def unpack_kernel(core_ref, mine_ref, other_ref, q_ref, k_ref, v_ref, o_ref):
    core = core_ref[0]
    mine = mine_ref[...].astype(f32)
    other = other_ref[...].astype(f32)
    k_ref[...] = jnp.where(core == 0, mine[:96], other[:96])
    v_ref[...] = jnp.where(core == 0, other[:96], mine[:96])
    for half, part in ((core, mine), (1 - core, other)):
        for b in range(2):
            rows = [part[96 + 96 * y + 48 * b : 144 + 96 * y + 48 * b] for y in range(4)]
            q_ref[:, pl.ds(pl.multiple_of(half * 256 + b * E, E), E)] = jnp.concatenate(rows[:2], axis=0)
            rows = jnp.concatenate(rows[2:], axis=0)
            for cb in range(3):
                o_ref[:, pl.ds(pl.multiple_of(half * 768 + cb * 256 + b * E, E), E)] = rows[
                    cb * 32 : cb * 32 + 32
                ]


def unpack(core, mine, other):
    return pl.pallas_call(
        unpack_kernel,
        out_shape=(
            jax.ShapeDtypeStruct((96, 512), f32),
            jax.ShapeDtypeStruct((96, E), f32),
            jax.ShapeDtypeStruct((96, E), f32),
            jax.ShapeDtypeStruct((32, 1536), f32),
        ),
        in_specs=[SMEM] + vmem_specs(2),
        out_specs=tuple(vmem_specs(4)),
        cost_estimate=pl.CostEstimate(flops=mine.size, bytes_accessed=mine.size * 12, transcendentals=0),
    )(core, mine, other)


def after(value, *others):
    return lax.optimization_barrier((value, others))[0]


def swap(value, axis, k, size):
    return lax.ppermute(value, axis, [(i, i ^ k) for i in range(size)])


def core_swap(value):
    return swap(value, CORE, 1, 2)


def tree_sum(values):
    values = [value.astype(f32) for value in values]
    while len(values) > 1:
        values = [a + b for a, b in zip(values[::2], values[1::2])]
    return values[0]


def shards(activations, query_weight, key_weight, value_weight, output_weight, cotangent):
    inputs = activations[0]
    upstream = cotangent[0]
    rows = inputs.shape[0]
    core = lax.axis_index(CORE)
    x = lax.axis_index(X)
    zh = lax.axis_index(ZH)

    scalar = core.astype(jnp.int32)[None]

    y = lax.axis_index(Y)
    place = jnp.stack([x, zh, core, y]).astype(jnp.int32)

    piece = pack(place, query_weight, key_weight, value_weight, output_weight)
    inputs_next = core_swap(inputs)
    upstream_next = core_swap(upstream)
    pieces = [piece] + [swap(piece, ZH, k, 4) for k in range(1, 4)]
    kv_block = jnp.stack([jnp.concatenate([p[:48, :E], p[:48, E:]], axis=0) for p in pieces])
    qo_block = jnp.stack([p[48:] for p in pieces])
    qo_block, kv_block = after((qo_block, kv_block), inputs_next, upstream_next)
    kv_blocks = [kv_block] + [swap(kv_block, X, k, 4) for k in range(1, 4)]
    block = jnp.stack([qo_block] + [swap(qo_block, Y, k, 4) for k in range(1, 4)])
    blocks = [block] + [swap(block, X, k, 4) for k in range(1, 4)]

    w_kv, kv = keys_or_values(place, inputs, inputs_next, kv_blocks)
    kv = after(kv, block)
    kv_mine = lax.all_to_all(kv, RING, 0, 0).reshape(16 * rows, E)
    kv_other = core_swap(kv_mine)

    other_blocks = [core_swap(block) for block in blocks]
    w_q, w_o, queries, d_att, inputs_t = prepare(
        place, inputs, inputs_next, upstream, upstream_next, blocks, other_blocks
    )
    w_all = jnp.concatenate([w_q, w_kv, core_swap(w_kv)], axis=1)

    attended, d_query, kept, sent = attention(scalar, queries, kv_mine, kv_other, d_att)

    attended_other = core_swap(attended)
    terms = grads(scalar, inputs_t, upstream, upstream_next, d_query, attended, attended_other)
    x_terms = [lax.dynamic_slice(terms, ((x ^ k) * 4, 0, 0), (4, 192, 256)) for k in range(4)]

    d_kv = (kept.astype(f32) + core_swap(after(sent, attended_other)).astype(f32)).astype(bf16).reshape(8, 2 * rows, E)
    d_kv = lax.all_to_all(after(d_kv, x_terms), RING, 0, 0)
    x_got = [x_terms[0]] + [swap(x_terms[k], X, k, 4) for k in range(1, 4)]
    d_kv, x_got = lax.optimization_barrier((d_kv, x_got))
    d_mine = jnp.sum(d_kv.astype(f32), axis=0).astype(bf16)

    d_own = lax.dynamic_slice(d_mine, (core * rows, 0), (rows, E))
    d_next = lax.dynamic_slice(d_mine, ((1 - core) * rows, 0), (rows, E))
    kv_grad = dot(inputs_t, jnp.concatenate([d_own, d_next], axis=0), NN).astype(bf16)
    kv_terms = [lax.dynamic_slice(kv_grad, ((x ^ k) * 384, 0), (384, E)) for k in range(4)]
    terms = tree_sum(x_got).astype(bf16)
    y_terms = [lax.dynamic_slice(terms, (0, (y ^ k) * 48, 0), (4, 48, 256)) for k in range(4)]
    qo_sum = tree_sum([y_terms[0]] + [swap(y_terms[k], Y, k, 4) for k in range(1, 4)]).astype(bf16)
    kv_sum = tree_sum([kv_terms[0]] + [swap(kv_terms[k], X, k, 4) for k in range(1, 4)]).astype(bf16)
    terms = jnp.concatenate([kv_sum.reshape(4, 96, E), qo_sum[:, :, :E], qo_sum[:, :, E:]], axis=1)
    z_terms = [lax.dynamic_index_in_dim(terms, zh ^ k, 0, keepdims=False) for k in range(4)]
    share = tree_sum([z_terms[0]] + [swap(z_terms[k], ZH, k, 4) for k in range(1, 4)]).astype(bf16)

    w_o_mine = lax.dynamic_slice(w_o, (core * 256, 0), (256, 1536))
    w_o_other = lax.dynamic_slice(w_o, ((1 - core) * 256, 0), (256, 1536))
    layer_out = dot(
        jnp.concatenate([attended[:rows], attended_other[rows:]], axis=1),
        jnp.concatenate([w_o_mine, w_o_other], axis=0),
        NN,
    ).astype(bf16)
    d_all = jnp.concatenate([d_query[:rows], core_swap(d_query[rows:]), d_own, core_swap(d_next)], axis=1)
    input_grad = dot(d_all, w_all, NT).astype(bf16)
    terms = after(lax.all_to_all(jnp.broadcast_to(share[None], (8, 192, E)), RING, 0, 0), layer_out, input_grad)
    terms = terms.astype(f32)
    kv_sum = jnp.sum(terms[:, :96], axis=0)
    qo_sum = (terms[:4, 96:] + terms[4:, 96:]).reshape(384, E)
    final = lax.optimization_barrier(jnp.concatenate([kv_sum, qo_sum], axis=0).astype(bf16))
    query_grad, key_grad, value_grad, output_grad = unpack(scalar, final, core_swap(final))

    return (layer_out[None], input_grad[None], query_grad, key_grad, value_grad, output_grad)


def solution(mesh):
    split = Mesh(mesh.devices.reshape(2, 4, 2, 4, 4), (ZL, Y, CORE, X, ZH))
    seq = (ZL, Y, CORE)
    return jax.shard_map(
        shards,
        mesh=split,
        in_specs=(
            P(FSDP, seq, None),
            P(FSDP, None),
            P(FSDP, None),
            P(FSDP, None),
            P(FSDP, None),
            P(FSDP, seq, None),
        ),
        out_specs=(
            P(FSDP, seq, None),
            P(FSDP, seq, None),
            P(FSDP, None),
            P(FSDP, None),
            P(FSDP, None),
            P(FSDP, None),
        ),
        check_vma=False,
    )
```

```python
import math

import jax
import jax.numpy as jnp
from jax import lax
from jax.experimental import pallas as pl
from jax.experimental.pallas import tpu as pltpu
from jax.sharding import Mesh, PartitionSpec as P

f32 = jnp.float32
bf16 = jnp.bfloat16

NT = (((1,), (1,)), ((), ()))
NN = (((1,), (0,)), ((), ()))
TN = (((0,), (0,)), ((), ()))

E = 128
R = 256
C = 2048

ZL, Y, CORE, X, ZH = "zl", "y", "core", "x", "zh"
FSDP = (X, ZH)
RING = (ZL, Y)


def dot(a, b, dims):
    return lax.dot_general(a, b, dims, preferred_element_type=f32)


def start(pairs, sems):
    copies = [pltpu.make_async_copy(src, dst, sems.at[n]) for n, (src, dst) in enumerate(pairs)]
    for copy in copies:
        copy.start()
    return copies


def fetch(pairs, sems):
    for copy in start(pairs, sems):
        copy.wait()


def attention_kernel(
    core_ref, q_ref, mine_ref, other_ref, do_ref,
    att_ref, dq_ref, kept_ref, sent_ref,
    k_ref, v_ref, s_ref, e_ref, acc_ref, sems,
):
    length = k_ref.shape[0]
    rows, width = q_ref.shape
    scale = 1.0 / math.sqrt(E)
    scale2 = scale * math.log2(math.e)
    first = core_ref[0] == 0

    @pl.when(first)
    def _():
        fetch([(mine_ref, k_ref), (other_ref, v_ref)], sems)

    @pl.when(jnp.logical_not(first))
    def _():
        fetch([(other_ref, k_ref), (mine_ref, v_ref)], sems)

    blocks = [(r, h) for h in range(width // E) for r in range(rows // R)]
    for n, (r, h) in enumerate(blocks):
        at = (slice(r * R, (r + 1) * R), slice(h * E, (h + 1) * E))
        q = q_ref[at]
        top = jnp.full((R, E), -jnp.inf, f32)
        for i in range(length // C):
            part = slice(i * C, (i + 1) * C)
            s = dot(q, k_ref[part, :], NT)
            s_ref[:, part] = s
            for t in range(C // E):
                top = jnp.maximum(top, s[:, t * E : (t + 1) * E])
        top = jnp.max(top, axis=1, keepdims=True) * scale2
        total = jnp.zeros((R, E), f32)
        out = jnp.zeros((R, E), f32)
        for i in range(length // C):
            part = slice(i * C, (i + 1) * C)
            e = jnp.exp2(s_ref[:, part] * scale2 - top)
            for t in range(C // E):
                total = total + e[:, t * E : (t + 1) * E]
            eb = e.astype(bf16)
            e_ref[:, part] = eb
            out = out + dot(eb, v_ref[part, :], NN)
        inverse = 1.0 / jnp.sum(total, axis=1, keepdims=True)
        out = out * inverse
        att_ref[at] = out.astype(bf16)
        do = (do_ref[at].astype(f32) * inverse).astype(bf16)
        delta = jnp.sum(do.astype(f32) * out, axis=1, keepdims=True)
        dq = jnp.zeros((R, E), f32)
        q_t = q.T
        do_t = do.T
        for i in range(length // C):
            part = slice(i * C, (i + 1) * C)
            dp = dot(do, v_ref[part, :], NT)
            eb = e_ref[:, part]
            ds = (eb.astype(f32) * (dp - delta)).astype(bf16)
            dk = dot(q_t, ds, NN)
            dv = dot(do_t, eb, NN)
            if n == 0:
                acc_ref[0:E, part] = dk
                acc_ref[E : 2 * E, part] = dv
            elif n < len(blocks) - 1:
                acc_ref[0:E, part] += dk
                acc_ref[E : 2 * E, part] += dv
            else:
                dk = (acc_ref[0:E, part] + dk) * scale
                dv = acc_ref[E : 2 * E, part] + dv
                kept_ref[part, :] = jnp.where(first, dk, dv).T.astype(bf16)
                sent_ref[part, :] = jnp.where(first, dv, dk).T.astype(bf16)
            dq = dq + dot(ds, k_ref[part, :], NN)
        dq_ref[at] = (dq * scale).astype(bf16)


def vmem_specs(n):
    return [pl.BlockSpec(memory_space=pltpu.VMEM)] * n


def any_specs(n):
    return [pl.BlockSpec(memory_space=pl.ANY)] * n


SMEM = pl.BlockSpec(memory_space=pltpu.SMEM)


def attention(core, queries, mine, other, d_att):
    rows, width = queries.shape
    length = mine.shape[0]
    query_like = jax.ShapeDtypeStruct(queries.shape, bf16)
    key_like = jax.ShapeDtypeStruct(mine.shape, bf16)
    return pl.pallas_call(
        attention_kernel,
        out_shape=(query_like, query_like, key_like, key_like),
        in_specs=[SMEM] + vmem_specs(1) + any_specs(2) + vmem_specs(1),
        out_specs=tuple(vmem_specs(4)),
        scratch_shapes=[
            pltpu.VMEM((length, E), bf16),
            pltpu.VMEM((length, E), bf16),
            pltpu.VMEM((R, length), f32),
            pltpu.VMEM((R, length), bf16),
            pltpu.VMEM((2 * E, length), f32),
            pltpu.SemaphoreType.DMA((2,)),
        ],
        compiler_params=pltpu.CompilerParams(vmem_limit_bytes=58 * 1024 * 1024),
        cost_estimate=pl.CostEstimate(
            flops=12 * rows * length * width,
            bytes_accessed=8 * 1024 * 1024,
            transcendentals=rows * length * (width // E),
        ),
    )(core, queries, mine, other, d_att)


def prepare_kernel(place_ref, x0_ref, x1_ref, u0_ref, u1_ref, *refs):
    arrived = refs[:8]
    wq_ref, wo_ref, q_ref, da_ref, x_ref, u_ref, blocks, sems = refs[8:]
    x, zh, core, y = place_ref[0], place_ref[1], place_ref[2], place_ref[3]
    copies = start(
        [
            (ref.at[ky], blocks.at[n, :, pl.ds(pl.multiple_of((y ^ ky) * 48, 16), 48), :])
            for n, ref in enumerate(arrived)
            for ky in range(4)
        ]
        + [(x0_ref, x_ref.at[:R]), (x1_ref, x_ref.at[R:]), (u0_ref, u_ref.at[:R]), (u1_ref, u_ref.at[R:])],
        sems,
    )
    for n in range(8):
        for ky in range(4):
            copies[n * 4 + ky].wait()
        side, k = n // 4, n % 4
        half = core ^ side
        for kz in range(4):
            shard = (x ^ k) * 4 + (zh ^ kz)
            wq_ref[pl.ds(pl.multiple_of(shard * 96, 32), 96), side * 256 : side * 256 + 256] = blocks[n, kz, :96, :]
            for cb in range(3):
                wo_ref[
                    pl.ds(pl.multiple_of(shard * 32, 32), 32),
                    pl.ds(pl.multiple_of(half * 768 + cb * 256, 256), 256),
                ] = blocks[n, kz, 96 + cb * 32 : 128 + cb * 32, :]
    for n in range(32, 36):
        copies[n].wait()
    q_ref[...] = dot(x_ref[...], wq_ref[:, :256], NN).astype(bf16)
    w_o = wo_ref[pl.ds(pl.multiple_of(core * 256, 256), 256), :]
    da_ref[...] = dot(u_ref[...], w_o, NT).astype(bf16)


def prepare(place, inputs, inputs_next, upstream, upstream_next, mine, other):
    rows, width = 2 * inputs.shape[0], inputs.shape[1]
    return pl.pallas_call(
        prepare_kernel,
        out_shape=(
            jax.ShapeDtypeStruct((width, 512), bf16),
            jax.ShapeDtypeStruct((512, width), bf16),
            jax.ShapeDtypeStruct((rows, 256), bf16),
            jax.ShapeDtypeStruct((rows, 256), bf16),
        ),
        in_specs=[SMEM] + any_specs(12),
        out_specs=tuple(vmem_specs(4)),
        scratch_shapes=[
            pltpu.VMEM((rows, width), bf16),
            pltpu.VMEM((rows, width), bf16),
            pltpu.VMEM((8, 4, 192, 256), bf16),
            pltpu.SemaphoreType.DMA((36,)),
        ],
        compiler_params=pltpu.CompilerParams(vmem_limit_bytes=58 * 1024 * 1024),
        cost_estimate=pl.CostEstimate(
            flops=80 * rows * width * 256, bytes_accessed=48 * 1024 * 1024, transcendentals=0
        ),
    )(place, inputs, inputs_next, upstream, upstream_next, *mine, *other)


def transpose_kernel(x0_ref, x1_ref, out_ref):
    out_ref[:, :R] = x0_ref[...].T
    out_ref[:, R:] = x1_ref[...].T


def transposed(inputs, inputs_next):
    rows, width = inputs.shape
    return pl.pallas_call(
        transpose_kernel,
        out_shape=jax.ShapeDtypeStruct((width, 2 * rows), bf16),
        in_specs=vmem_specs(2),
        out_specs=vmem_specs(1)[0],
        compiler_params=pltpu.CompilerParams(vmem_limit_bytes=58 * 1024 * 1024),
    )(inputs, inputs_next)


def pack_kernel(place_ref, q_ref, k_ref, v_ref, o_ref, out_ref, rows_ref):
    core, y = place_ref[2], place_ref[3]
    kv = jnp.where(core == 0, k_ref[...].astype(f32), v_ref[...].astype(f32)).astype(bf16)
    out_ref[:48, :E] = kv[:48]
    out_ref[:48, E:] = kv[48:]
    rows_ref[:96, :] = q_ref[:, pl.ds(pl.multiple_of(core * 256, 256), 256)]
    for cb in range(3):
        rows_ref[96 + cb * 32 : 128 + cb * 32, :] = o_ref[
            :, pl.ds(pl.multiple_of(core * 768 + cb * 256, 256), 256)
        ]
    out_ref[48:, :] = rows_ref[pl.ds(pl.multiple_of(y * 48, 16), 48), :]


def pack(place, *weights):
    return pl.pallas_call(
        pack_kernel,
        out_shape=jax.ShapeDtypeStruct((96, 256), bf16),
        in_specs=[SMEM] + vmem_specs(4),
        out_specs=vmem_specs(1)[0],
        scratch_shapes=[pltpu.VMEM((192, 256), bf16)],
    )(place, *weights)


def kv_kernel(place_ref, x0_ref, x1_ref, w0, w1, w2, w3, w_ref, out_ref, x_ref, blocks, sems):
    x, zh, core = place_ref[0], place_ref[1], place_ref[2]
    copies = start(
        [(ref, blocks.at[k]) for k, ref in enumerate((w0, w1, w2, w3))]
        + [(x0_ref, x_ref.at[:R]), (x1_ref, x_ref.at[R:])],
        sems,
    )
    for k in range(4):
        copies[k].wait()
        for kz in range(4):
            first_row = ((x ^ k) * 4 + (zh ^ kz)) * 96
            w_ref[pl.ds(pl.multiple_of(first_row, 32), 96), :] = blocks[k, kz]
    copies[4].wait()
    copies[5].wait()
    for n, owner in enumerate((core, 1 - core)):
        kv = dot(x_ref[n * R : (n + 1) * R, :], w_ref[...], NN).astype(bf16)
        for chip in range(8):
            out_ref[chip, pl.ds(pl.multiple_of(owner * R, R), R), :] = kv


def keys_or_values(place, inputs, inputs_next, blocks):
    rows, width = inputs.shape
    return pl.pallas_call(
        kv_kernel,
        out_shape=(
            jax.ShapeDtypeStruct((width, E), bf16),
            jax.ShapeDtypeStruct((8, 2 * rows, E), bf16),
        ),
        in_specs=[SMEM] + any_specs(6),
        out_specs=tuple(vmem_specs(2)),
        scratch_shapes=[
            pltpu.VMEM((2 * rows, width), bf16),
            pltpu.VMEM((4, 4, 96, E), bf16),
            pltpu.SemaphoreType.DMA((6,)),
        ],
        compiler_params=pltpu.CompilerParams(vmem_limit_bytes=58 * 1024 * 1024),
        cost_estimate=pl.CostEstimate(
            flops=4 * rows * width * E, bytes_accessed=4 * 1024 * 1024, transcendentals=0
        ),
    )(place, inputs, inputs_next, *blocks)


def grads_kernel(place_ref, xt_hbm, u0_hbm, u1_hbm, dq_hbm, att_hbm, other_hbm, *refs):
    outs = refs[:4]
    xt_ref, u_ref, small, out_ref, sems, out_sems = refs[4:]
    x, core = place_ref[0], place_ref[2]
    half = pl.ds(pl.multiple_of(core * 768, 256), 768)
    copies = start(
        [
            (att_hbm, small.at[0]),
            (other_hbm.at[:R], small.at[1, R:]),
            (other_hbm.at[R:], small.at[1, :R]),
            (u0_hbm.at[:, half], u_ref.at[:R]),
            (u1_hbm.at[:, half], u_ref.at[R:]),
            (dq_hbm, small.at[2]),
            (xt_hbm, xt_ref),
        ],
        sems,
    )
    for n in range(5):
        copies[n].wait()
    for n, owner in enumerate((core, 1 - core)):
        att = small[n].T
        for cb in range(3):
            o_grad = dot(att, u_ref[:, cb * 256 : (cb + 1) * 256], NN).astype(bf16).reshape(8, 32, 256)
            out_ref[pl.ds(owner * 8, 8), 96 + cb * 32 : 128 + cb * 32, :] = o_grad
    copies[5].wait()
    copies[6].wait()
    for g in range(4):
        q_grad = dot(xt_ref[g * 384 : (g + 1) * 384, :], small[2], NN).astype(bf16)
        out_ref[g * 4 : (g + 1) * 4, 0:96, :] = q_grad.reshape(4, 96, 256)
    fetch([(out_ref.at[pl.ds((x ^ k) * 4, 4)], out) for k, out in enumerate(outs)], out_sems)


def grads(place, inputs_t, upstream, upstream_next, d_query, attended, other):
    return pl.pallas_call(
        grads_kernel,
        out_shape=(jax.ShapeDtypeStruct((4, 192, 256), bf16),) * 4,
        in_specs=[SMEM] + any_specs(6),
        out_specs=tuple(any_specs(4)),
        scratch_shapes=[
            pltpu.VMEM(inputs_t.shape, bf16),
            pltpu.VMEM((2 * R, 768), bf16),
            pltpu.VMEM((3, 2 * R, 256), bf16),
            pltpu.VMEM((16, 192, 256), bf16),
            pltpu.SemaphoreType.DMA((7,)),
            pltpu.SemaphoreType.DMA((4,)),
        ],
        compiler_params=pltpu.CompilerParams(vmem_limit_bytes=58 * 1024 * 1024),
        cost_estimate=pl.CostEstimate(
            flops=4 * inputs_t.size * 256, bytes_accessed=6 * 1024 * 1024, transcendentals=0
        ),
    )(place, inputs_t, upstream, upstream_next, d_query, attended, other)


def unpack_kernel(core_ref, mine_ref, other_ref, q_ref, k_ref, v_ref, o_ref):
    core = core_ref[0]
    mine = mine_ref[...].astype(f32)
    other = other_ref[...].astype(f32)
    k_ref[...] = jnp.where(core == 0, mine[:96], other[:96])
    v_ref[...] = jnp.where(core == 0, other[:96], mine[:96])
    for half, part in ((core, mine), (1 - core, other)):
        for b in range(2):
            rows = [part[96 + 96 * y + 48 * b : 144 + 96 * y + 48 * b] for y in range(4)]
            q_ref[:, pl.ds(pl.multiple_of(half * 256 + b * E, E), E)] = jnp.concatenate(rows[:2], axis=0)
            rows = jnp.concatenate(rows[2:], axis=0)
            for cb in range(3):
                o_ref[:, pl.ds(pl.multiple_of(half * 768 + cb * 256 + b * E, E), E)] = rows[
                    cb * 32 : cb * 32 + 32
                ]


def unpack(core, mine, other):
    return pl.pallas_call(
        unpack_kernel,
        out_shape=(
            jax.ShapeDtypeStruct((96, 512), f32),
            jax.ShapeDtypeStruct((96, E), f32),
            jax.ShapeDtypeStruct((96, E), f32),
            jax.ShapeDtypeStruct((32, 1536), f32),
        ),
        in_specs=[SMEM] + vmem_specs(2),
        out_specs=tuple(vmem_specs(4)),
        cost_estimate=pl.CostEstimate(flops=mine.size, bytes_accessed=mine.size * 12, transcendentals=0),
    )(core, mine, other)


def after(value, *others):
    return lax.optimization_barrier((value, others))[0]


def swap(value, axis, k, size):
    return lax.ppermute(value, axis, [(i, i ^ k) for i in range(size)])


def core_swap(value):
    return swap(value, CORE, 1, 2)


def tree_sum(values):
    values = [value.astype(f32) for value in values]
    while len(values) > 1:
        values = [a + b for a, b in zip(values[::2], values[1::2])]
    return values[0]


def shards(activations, query_weight, key_weight, value_weight, output_weight, cotangent):
    inputs = activations[0]
    upstream = cotangent[0]
    rows = inputs.shape[0]
    core = lax.axis_index(CORE)
    x = lax.axis_index(X)
    zh = lax.axis_index(ZH)

    scalar = core.astype(jnp.int32)[None]

    y = lax.axis_index(Y)
    place = jnp.stack([x, zh, core, y]).astype(jnp.int32)

    piece = pack(place, query_weight, key_weight, value_weight, output_weight)
    inputs_next = core_swap(inputs)
    upstream_next = core_swap(upstream)
    pieces = [piece] + [swap(piece, ZH, k, 4) for k in range(1, 4)]
    kv_block = jnp.stack([jnp.concatenate([p[:48, :E], p[:48, E:]], axis=0) for p in pieces])
    qo_block = jnp.stack([p[48:] for p in pieces])
    qo_block, kv_block = after((qo_block, kv_block), inputs_next, upstream_next)
    kv_blocks = [kv_block] + [swap(kv_block, X, k, 4) for k in range(1, 4)]
    block = jnp.stack([qo_block] + [swap(qo_block, Y, k, 4) for k in range(1, 4)])
    blocks = [block] + [swap(block, X, k, 4) for k in range(1, 4)]

    inputs_t = transposed(inputs, inputs_next)
    kv_blocks = after(kv_blocks, inputs_t)
    w_kv, kv = keys_or_values(place, inputs, inputs_next, kv_blocks)
    kv = after(kv, block)
    kv_mine = lax.all_to_all(kv, RING, 0, 0).reshape(16 * rows, E)
    kv_other = core_swap(kv_mine)

    other_blocks = [core_swap(block) for block in blocks]
    w_q, w_o, queries, d_att = prepare(
        place, inputs, inputs_next, upstream, upstream_next, blocks, other_blocks
    )
    w_all = jnp.concatenate([w_q, w_kv, core_swap(w_kv)], axis=1)

    attended, d_query, kept, sent = attention(scalar, queries, kv_mine, kv_other, d_att)

    attended_other = core_swap(attended)
    x_terms = grads(place, inputs_t, upstream, upstream_next, d_query, attended, attended_other)

    d_kv = (kept.astype(f32) + core_swap(after(sent, attended_other)).astype(f32)).astype(bf16).reshape(8, 2 * rows, E)
    d_kv = lax.all_to_all(after(d_kv, x_terms), RING, 0, 0)
    x_got = [x_terms[0]] + [swap(x_terms[k], X, k, 4) for k in range(1, 4)]
    d_kv, x_got = lax.optimization_barrier((d_kv, x_got))
    d_mine = jnp.sum(d_kv.astype(f32), axis=0).astype(bf16)

    d_own = lax.dynamic_slice(d_mine, (core * rows, 0), (rows, E))
    d_next = lax.dynamic_slice(d_mine, ((1 - core) * rows, 0), (rows, E))
    kv_grad = dot(inputs_t, jnp.concatenate([d_own, d_next], axis=0), NN).astype(bf16)
    kv_terms = [lax.dynamic_slice(kv_grad, ((x ^ k) * 384, 0), (384, E)) for k in range(4)]
    terms = tree_sum(x_got).astype(bf16)
    y_terms = [lax.dynamic_slice(terms, (0, (y ^ k) * 48, 0), (4, 48, 256)) for k in range(4)]
    qo_sum = tree_sum([y_terms[0]] + [swap(y_terms[k], Y, k, 4) for k in range(1, 4)]).astype(bf16)
    kv_sum = tree_sum([kv_terms[0]] + [swap(kv_terms[k], X, k, 4) for k in range(1, 4)]).astype(bf16)
    terms = jnp.concatenate([kv_sum.reshape(4, 96, E), qo_sum[:, :, :E], qo_sum[:, :, E:]], axis=1)
    z_terms = [lax.dynamic_index_in_dim(terms, zh ^ k, 0, keepdims=False) for k in range(4)]
    share = tree_sum([z_terms[0]] + [swap(z_terms[k], ZH, k, 4) for k in range(1, 4)]).astype(bf16)

    w_o_mine = lax.dynamic_slice(w_o, (core * 256, 0), (256, 1536))
    w_o_other = lax.dynamic_slice(w_o, ((1 - core) * 256, 0), (256, 1536))
    layer_out = dot(
        jnp.concatenate([attended[:rows], attended_other[rows:]], axis=1),
        jnp.concatenate([w_o_mine, w_o_other], axis=0),
        NN,
    ).astype(bf16)
    d_all = jnp.concatenate([d_query[:rows], core_swap(d_query[rows:]), d_own, core_swap(d_next)], axis=1)
    input_grad = dot(d_all, w_all, NT).astype(bf16)
    terms = after(lax.all_to_all(jnp.broadcast_to(share[None], (8, 192, E)), RING, 0, 0), layer_out, input_grad)
    terms = terms.astype(f32)
    kv_sum = jnp.sum(terms[:, :96], axis=0)
    qo_sum = (terms[:4, 96:] + terms[4:, 96:]).reshape(384, E)
    final = lax.optimization_barrier(jnp.concatenate([kv_sum, qo_sum], axis=0).astype(bf16))
    query_grad, key_grad, value_grad, output_grad = unpack(scalar, final, core_swap(final))

    return (layer_out[None], input_grad[None], query_grad, key_grad, value_grad, output_grad)


def solution(mesh):
    split = Mesh(mesh.devices.reshape(2, 4, 2, 4, 4), (ZL, Y, CORE, X, ZH))
    seq = (ZL, Y, CORE)
    return jax.shard_map(
        shards,
        mesh=split,
        in_specs=(
            P(FSDP, seq, None),
            P(FSDP, None),
            P(FSDP, None),
            P(FSDP, None),
            P(FSDP, None),
            P(FSDP, seq, None),
        ),
        out_specs=(
            P(FSDP, seq, None),
            P(FSDP, seq, None),
            P(FSDP, None),
            P(FSDP, None),
            P(FSDP, None),
            P(FSDP, None),
        ),
        check_vma=False,
    )
```

```python
import math

import jax
import jax.numpy as jnp
from jax import lax
from jax.experimental import pallas as pl
from jax.experimental.pallas import tpu as pltpu
from jax.sharding import Mesh, PartitionSpec as P

f32 = jnp.float32
bf16 = jnp.bfloat16

NT = (((1,), (1,)), ((), ()))
NN = (((1,), (0,)), ((), ()))
TN = (((0,), (0,)), ((), ()))

E = 128
R = 256
C = 4096

ZL, Y, CORE, X, ZH = "zl", "y", "core", "x", "zh"
FSDP = (X, ZH)
RING = (ZL, Y)


def dot(a, b, dims):
    return lax.dot_general(a, b, dims, preferred_element_type=f32)


def start(pairs, sems):
    copies = [pltpu.make_async_copy(src, dst, sems.at[n]) for n, (src, dst) in enumerate(pairs)]
    for copy in copies:
        copy.start()
    return copies


def fetch(pairs, sems):
    for copy in start(pairs, sems):
        copy.wait()


def attention_kernel(
    core_ref, q_ref, mine_ref, other_ref, do_ref,
    att_ref, dq_ref, kept_ref, sent_ref,
    k_ref, v_ref, s_ref, e_ref, acc_ref, sems,
):
    length = k_ref.shape[0]
    rows, width = q_ref.shape
    scale = 1.0 / math.sqrt(E)
    scale2 = scale * math.log2(math.e)
    first = core_ref[0] == 0

    @pl.when(first)
    def _():
        fetch([(mine_ref, k_ref), (other_ref, v_ref)], sems)

    @pl.when(jnp.logical_not(first))
    def _():
        fetch([(other_ref, k_ref), (mine_ref, v_ref)], sems)

    blocks = [(r, h) for h in range(width // E) for r in range(rows // R)]
    for n, (r, h) in enumerate(blocks):
        at = (slice(r * R, (r + 1) * R), slice(h * E, (h + 1) * E))
        q = q_ref[at]
        top = jnp.full((R, E), -jnp.inf, f32)
        for i in range(length // C):
            part = slice(i * C, (i + 1) * C)
            s = dot(q, k_ref[part, :], NT)
            s_ref[:, part] = s
            for t in range(C // E):
                top = jnp.maximum(top, s[:, t * E : (t + 1) * E])
        top = jnp.max(top, axis=1, keepdims=True) * scale2
        total = jnp.zeros((R, E), f32)
        out = jnp.zeros((R, E), f32)
        for i in range(length // C):
            part = slice(i * C, (i + 1) * C)
            e = jnp.exp2(s_ref[:, part] * scale2 - top)
            for t in range(C // E):
                total = total + e[:, t * E : (t + 1) * E]
            eb = e.astype(bf16)
            e_ref[:, part] = eb
            out = out + dot(eb, v_ref[part, :], NN)
        inverse = 1.0 / jnp.sum(total, axis=1, keepdims=True)
        out = out * inverse
        att_ref[at] = out.astype(bf16)
        do = (do_ref[at].astype(f32) * inverse).astype(bf16)
        delta = jnp.sum(do.astype(f32) * out, axis=1, keepdims=True)
        dq = jnp.zeros((R, E), f32)
        q_t = q.T
        do_t = do.T
        for i in range(length // C):
            part = slice(i * C, (i + 1) * C)
            dp = dot(do, v_ref[part, :], NT)
            eb = e_ref[:, part]
            ds = (eb.astype(f32) * (dp - delta)).astype(bf16)
            dk = dot(q_t, ds, NN)
            dv = dot(do_t, eb, NN)
            if n == 0:
                acc_ref[0:E, part] = dk
                acc_ref[E : 2 * E, part] = dv
            elif n < len(blocks) - 1:
                acc_ref[0:E, part] += dk
                acc_ref[E : 2 * E, part] += dv
            else:
                dk = (acc_ref[0:E, part] + dk) * scale
                dv = acc_ref[E : 2 * E, part] + dv
                kept_ref[part, :] = jnp.where(first, dk, dv).T.astype(bf16)
                sent_ref[part, :] = jnp.where(first, dv, dk).T.astype(bf16)
            dq = dq + dot(ds, k_ref[part, :], NN)
        dq_ref[at] = (dq * scale).astype(bf16)


def vmem_specs(n):
    return [pl.BlockSpec(memory_space=pltpu.VMEM)] * n


def any_specs(n):
    return [pl.BlockSpec(memory_space=pl.ANY)] * n


SMEM = pl.BlockSpec(memory_space=pltpu.SMEM)


def attention(core, queries, mine, other, d_att):
    rows, width = queries.shape
    length = mine.shape[0]
    query_like = jax.ShapeDtypeStruct(queries.shape, bf16)
    key_like = jax.ShapeDtypeStruct(mine.shape, bf16)
    return pl.pallas_call(
        attention_kernel,
        out_shape=(query_like, query_like, key_like, key_like),
        in_specs=[SMEM] + vmem_specs(1) + any_specs(2) + vmem_specs(1),
        out_specs=tuple(vmem_specs(4)),
        scratch_shapes=[
            pltpu.VMEM((length, E), bf16),
            pltpu.VMEM((length, E), bf16),
            pltpu.VMEM((R, length), f32),
            pltpu.VMEM((R, length), bf16),
            pltpu.VMEM((2 * E, length), f32),
            pltpu.SemaphoreType.DMA((2,)),
        ],
        compiler_params=pltpu.CompilerParams(vmem_limit_bytes=58 * 1024 * 1024),
        cost_estimate=pl.CostEstimate(
            flops=12 * rows * length * width,
            bytes_accessed=8 * 1024 * 1024,
            transcendentals=rows * length * (width // E),
        ),
    )(core, queries, mine, other, d_att)


def prepare_kernel(place_ref, x0_ref, x1_ref, u0_ref, u1_ref, *refs):
    arrived = refs[:8]
    wq_ref, wo_ref, q_ref, da_ref, x_ref, u_ref, blocks, sems = refs[8:]
    x, zh, core, y = place_ref[0], place_ref[1], place_ref[2], place_ref[3]
    copies = start(
        [
            (ref.at[ky], blocks.at[n, :, pl.ds(pl.multiple_of((y ^ ky) * 48, 16), 48), :])
            for n, ref in enumerate(arrived)
            for ky in range(4)
        ]
        + [(x0_ref, x_ref.at[:R]), (x1_ref, x_ref.at[R:]), (u0_ref, u_ref.at[:R]), (u1_ref, u_ref.at[R:])],
        sems,
    )
    for n in range(8):
        for ky in range(4):
            copies[n * 4 + ky].wait()
        side, k = n // 4, n % 4
        half = core ^ side
        for kz in range(4):
            shard = (x ^ k) * 4 + (zh ^ kz)
            wq_ref[pl.ds(pl.multiple_of(shard * 96, 32), 96), side * 256 : side * 256 + 256] = blocks[n, kz, :96, :]
            for cb in range(3):
                wo_ref[
                    pl.ds(pl.multiple_of(shard * 32, 32), 32),
                    pl.ds(pl.multiple_of(half * 768 + cb * 256, 256), 256),
                ] = blocks[n, kz, 96 + cb * 32 : 128 + cb * 32, :]
    for n in range(32, 36):
        copies[n].wait()
    q_ref[...] = dot(x_ref[...], wq_ref[:, :256], NN).astype(bf16)
    w_o = wo_ref[pl.ds(pl.multiple_of(core * 256, 256), 256), :]
    da_ref[...] = dot(u_ref[...], w_o, NT).astype(bf16)


def prepare(place, inputs, inputs_next, upstream, upstream_next, mine, other):
    rows, width = 2 * inputs.shape[0], inputs.shape[1]
    return pl.pallas_call(
        prepare_kernel,
        out_shape=(
            jax.ShapeDtypeStruct((width, 512), bf16),
            jax.ShapeDtypeStruct((512, width), bf16),
            jax.ShapeDtypeStruct((rows, 256), bf16),
            jax.ShapeDtypeStruct((rows, 256), bf16),
        ),
        in_specs=[SMEM] + any_specs(12),
        out_specs=tuple(vmem_specs(4)),
        scratch_shapes=[
            pltpu.VMEM((rows, width), bf16),
            pltpu.VMEM((rows, width), bf16),
            pltpu.VMEM((8, 4, 192, 256), bf16),
            pltpu.SemaphoreType.DMA((36,)),
        ],
        compiler_params=pltpu.CompilerParams(vmem_limit_bytes=58 * 1024 * 1024),
        cost_estimate=pl.CostEstimate(
            flops=80 * rows * width * 256, bytes_accessed=48 * 1024 * 1024, transcendentals=0
        ),
    )(place, inputs, inputs_next, upstream, upstream_next, *mine, *other)


def transpose_kernel(x0_ref, x1_ref, out_ref):
    out_ref[:, :R] = x0_ref[...].T
    out_ref[:, R:] = x1_ref[...].T


def transposed(inputs, inputs_next):
    rows, width = inputs.shape
    return pl.pallas_call(
        transpose_kernel,
        out_shape=jax.ShapeDtypeStruct((width, 2 * rows), bf16),
        in_specs=vmem_specs(2),
        out_specs=vmem_specs(1)[0],
        compiler_params=pltpu.CompilerParams(vmem_limit_bytes=58 * 1024 * 1024),
    )(inputs, inputs_next)


def pack_kernel(place_ref, q_ref, k_ref, v_ref, o_ref, out_ref, rows_ref):
    core, y = place_ref[2], place_ref[3]
    kv = jnp.where(core == 0, k_ref[...].astype(f32), v_ref[...].astype(f32)).astype(bf16)
    out_ref[:48, :E] = kv[:48]
    out_ref[:48, E:] = kv[48:]
    rows_ref[:96, :] = q_ref[:, pl.ds(pl.multiple_of(core * 256, 256), 256)]
    for cb in range(3):
        rows_ref[96 + cb * 32 : 128 + cb * 32, :] = o_ref[
            :, pl.ds(pl.multiple_of(core * 768 + cb * 256, 256), 256)
        ]
    out_ref[48:, :] = rows_ref[pl.ds(pl.multiple_of(y * 48, 16), 48), :]


def pack(place, *weights):
    return pl.pallas_call(
        pack_kernel,
        out_shape=jax.ShapeDtypeStruct((96, 256), bf16),
        in_specs=[SMEM] + vmem_specs(4),
        out_specs=vmem_specs(1)[0],
        scratch_shapes=[pltpu.VMEM((192, 256), bf16)],
    )(place, *weights)


def kv_kernel(place_ref, x0_ref, x1_ref, w0, w1, w2, w3, w_ref, out_ref, x_ref, blocks, sems):
    x, zh, core = place_ref[0], place_ref[1], place_ref[2]
    copies = start(
        [(ref, blocks.at[k]) for k, ref in enumerate((w0, w1, w2, w3))]
        + [(x0_ref, x_ref.at[:R]), (x1_ref, x_ref.at[R:])],
        sems,
    )
    for k in range(4):
        copies[k].wait()
        for kz in range(4):
            first_row = ((x ^ k) * 4 + (zh ^ kz)) * 96
            w_ref[pl.ds(pl.multiple_of(first_row, 32), 96), :] = blocks[k, kz]
    copies[4].wait()
    copies[5].wait()
    for n, owner in enumerate((core, 1 - core)):
        kv = dot(x_ref[n * R : (n + 1) * R, :], w_ref[...], NN).astype(bf16)
        for chip in range(8):
            out_ref[chip, pl.ds(pl.multiple_of(owner * R, R), R), :] = kv


def keys_or_values(place, inputs, inputs_next, blocks):
    rows, width = inputs.shape
    return pl.pallas_call(
        kv_kernel,
        out_shape=(
            jax.ShapeDtypeStruct((width, E), bf16),
            jax.ShapeDtypeStruct((8, 2 * rows, E), bf16),
        ),
        in_specs=[SMEM] + any_specs(6),
        out_specs=tuple(vmem_specs(2)),
        scratch_shapes=[
            pltpu.VMEM((2 * rows, width), bf16),
            pltpu.VMEM((4, 4, 96, E), bf16),
            pltpu.SemaphoreType.DMA((6,)),
        ],
        compiler_params=pltpu.CompilerParams(vmem_limit_bytes=58 * 1024 * 1024),
        cost_estimate=pl.CostEstimate(
            flops=4 * rows * width * E, bytes_accessed=4 * 1024 * 1024, transcendentals=0
        ),
    )(place, inputs, inputs_next, *blocks)


def grads_kernel(place_ref, xt_hbm, u0_hbm, u1_hbm, dq_hbm, att_hbm, other_hbm, *refs):
    outs = refs[:4]
    xt_ref, u_ref, small, out_ref, sems, out_sems = refs[4:]
    x, core = place_ref[0], place_ref[2]
    half = pl.ds(pl.multiple_of(core * 768, 256), 768)
    copies = start(
        [
            (att_hbm, small.at[0]),
            (other_hbm.at[:R], small.at[1, R:]),
            (other_hbm.at[R:], small.at[1, :R]),
            (u0_hbm.at[:, half], u_ref.at[:R]),
            (u1_hbm.at[:, half], u_ref.at[R:]),
            (dq_hbm, small.at[2]),
            (xt_hbm, xt_ref),
        ],
        sems,
    )
    for n in range(5):
        copies[n].wait()
    for n, owner in enumerate((core, 1 - core)):
        att = small[n].T
        for cb in range(3):
            o_grad = dot(att, u_ref[:, cb * 256 : (cb + 1) * 256], NN).astype(bf16).reshape(8, 32, 256)
            out_ref[pl.ds(owner * 8, 8), 96 + cb * 32 : 128 + cb * 32, :] = o_grad
    copies[5].wait()
    copies[6].wait()
    for g in range(4):
        q_grad = dot(xt_ref[g * 384 : (g + 1) * 384, :], small[2], NN).astype(bf16)
        out_ref[g * 4 : (g + 1) * 4, 0:96, :] = q_grad.reshape(4, 96, 256)
    fetch([(out_ref.at[pl.ds((x ^ k) * 4, 4)], out) for k, out in enumerate(outs)], out_sems)


def grads(place, inputs_t, upstream, upstream_next, d_query, attended, other):
    return pl.pallas_call(
        grads_kernel,
        out_shape=(jax.ShapeDtypeStruct((4, 192, 256), bf16),) * 4,
        in_specs=[SMEM] + any_specs(6),
        out_specs=tuple(any_specs(4)),
        scratch_shapes=[
            pltpu.VMEM(inputs_t.shape, bf16),
            pltpu.VMEM((2 * R, 768), bf16),
            pltpu.VMEM((3, 2 * R, 256), bf16),
            pltpu.VMEM((16, 192, 256), bf16),
            pltpu.SemaphoreType.DMA((7,)),
            pltpu.SemaphoreType.DMA((4,)),
        ],
        compiler_params=pltpu.CompilerParams(vmem_limit_bytes=58 * 1024 * 1024),
        cost_estimate=pl.CostEstimate(
            flops=4 * inputs_t.size * 256, bytes_accessed=6 * 1024 * 1024, transcendentals=0
        ),
    )(place, inputs_t, upstream, upstream_next, d_query, attended, other)


def unpack_kernel(core_ref, mine_ref, other_ref, q_ref, k_ref, v_ref, o_ref):
    core = core_ref[0]
    mine = mine_ref[...].astype(f32)
    other = other_ref[...].astype(f32)
    k_ref[...] = jnp.where(core == 0, mine[:96], other[:96])
    v_ref[...] = jnp.where(core == 0, other[:96], mine[:96])
    for half, part in ((core, mine), (1 - core, other)):
        for b in range(2):
            rows = [part[96 + 96 * y + 48 * b : 144 + 96 * y + 48 * b] for y in range(4)]
            q_ref[:, pl.ds(pl.multiple_of(half * 256 + b * E, E), E)] = jnp.concatenate(rows[:2], axis=0)
            rows = jnp.concatenate(rows[2:], axis=0)
            for cb in range(3):
                o_ref[:, pl.ds(pl.multiple_of(half * 768 + cb * 256 + b * E, E), E)] = rows[
                    cb * 32 : cb * 32 + 32
                ]


def unpack(core, mine, other):
    return pl.pallas_call(
        unpack_kernel,
        out_shape=(
            jax.ShapeDtypeStruct((96, 512), f32),
            jax.ShapeDtypeStruct((96, E), f32),
            jax.ShapeDtypeStruct((96, E), f32),
            jax.ShapeDtypeStruct((32, 1536), f32),
        ),
        in_specs=[SMEM] + vmem_specs(2),
        out_specs=tuple(vmem_specs(4)),
        cost_estimate=pl.CostEstimate(flops=mine.size, bytes_accessed=mine.size * 12, transcendentals=0),
    )(core, mine, other)


def after(value, *others):
    return lax.optimization_barrier((value, others))[0]


def swap(value, axis, k, size):
    return lax.ppermute(value, axis, [(i, i ^ k) for i in range(size)])


def core_swap(value):
    return swap(value, CORE, 1, 2)


def tree_sum(values):
    values = [value.astype(f32) for value in values]
    while len(values) > 1:
        values = [a + b for a, b in zip(values[::2], values[1::2])]
    return values[0]


def shards(activations, query_weight, key_weight, value_weight, output_weight, cotangent):
    inputs = activations[0]
    upstream = cotangent[0]
    rows = inputs.shape[0]
    core = lax.axis_index(CORE)
    x = lax.axis_index(X)
    zh = lax.axis_index(ZH)

    scalar = core.astype(jnp.int32)[None]

    y = lax.axis_index(Y)
    place = jnp.stack([x, zh, core, y]).astype(jnp.int32)

    piece = pack(place, query_weight, key_weight, value_weight, output_weight)
    inputs_next = core_swap(inputs)
    upstream_next = core_swap(upstream)
    pieces = [piece] + [swap(piece, ZH, k, 4) for k in range(1, 4)]
    kv_block = jnp.stack([jnp.concatenate([p[:48, :E], p[:48, E:]], axis=0) for p in pieces])
    qo_block = jnp.stack([p[48:] for p in pieces])
    qo_block, kv_block = after((qo_block, kv_block), inputs_next, upstream_next)
    kv_blocks = [kv_block] + [swap(kv_block, X, k, 4) for k in range(1, 4)]
    block = jnp.stack([qo_block] + [swap(qo_block, Y, k, 4) for k in range(1, 4)])
    blocks = [block] + [swap(block, X, k, 4) for k in range(1, 4)]

    inputs_t = transposed(inputs, inputs_next)
    kv_blocks = after(kv_blocks, inputs_t)
    w_kv, kv = keys_or_values(place, inputs, inputs_next, kv_blocks)
    kv = after(kv, block)
    kv_mine = lax.all_to_all(kv, RING, 0, 0).reshape(16 * rows, E)
    kv_other = core_swap(kv_mine)

    other_blocks = [core_swap(block) for block in blocks]
    w_q, w_o, queries, d_att = prepare(
        place, inputs, inputs_next, upstream, upstream_next, blocks, other_blocks
    )
    w_all = jnp.concatenate([w_q, w_kv, core_swap(w_kv)], axis=1)

    attended, d_query, kept, sent = attention(scalar, queries, kv_mine, kv_other, d_att)

    attended_other = core_swap(attended)
    x_terms = grads(place, inputs_t, upstream, upstream_next, d_query, attended, attended_other)

    d_kv = (kept.astype(f32) + core_swap(after(sent, attended_other)).astype(f32)).astype(bf16).reshape(8, 2 * rows, E)
    d_kv = lax.all_to_all(after(d_kv, x_terms), RING, 0, 0)
    x_got = [x_terms[0]] + [swap(x_terms[k], X, k, 4) for k in range(1, 4)]
    d_kv, x_got = lax.optimization_barrier((d_kv, x_got))
    d_mine = jnp.sum(d_kv.astype(f32), axis=0).astype(bf16)

    d_own = lax.dynamic_slice(d_mine, (core * rows, 0), (rows, E))
    d_next = lax.dynamic_slice(d_mine, ((1 - core) * rows, 0), (rows, E))
    kv_grad = dot(inputs_t, jnp.concatenate([d_own, d_next], axis=0), NN).astype(bf16)
    kv_terms = [lax.dynamic_slice(kv_grad, ((x ^ k) * 384, 0), (384, E)) for k in range(4)]
    terms = tree_sum(x_got).astype(bf16)
    y_terms = [lax.dynamic_slice(terms, (0, (y ^ k) * 48, 0), (4, 48, 256)) for k in range(4)]
    qo_sum = tree_sum([y_terms[0]] + [swap(y_terms[k], Y, k, 4) for k in range(1, 4)]).astype(bf16)
    kv_sum = tree_sum([kv_terms[0]] + [swap(kv_terms[k], X, k, 4) for k in range(1, 4)]).astype(bf16)
    terms = jnp.concatenate([kv_sum.reshape(4, 96, E), qo_sum[:, :, :E], qo_sum[:, :, E:]], axis=1)
    z_terms = [lax.dynamic_index_in_dim(terms, zh ^ k, 0, keepdims=False) for k in range(4)]
    share = tree_sum([z_terms[0]] + [swap(z_terms[k], ZH, k, 4) for k in range(1, 4)]).astype(bf16)

    w_o_mine = lax.dynamic_slice(w_o, (core * 256, 0), (256, 1536))
    w_o_other = lax.dynamic_slice(w_o, ((1 - core) * 256, 0), (256, 1536))
    layer_out = dot(
        jnp.concatenate([attended[:rows], attended_other[rows:]], axis=1),
        jnp.concatenate([w_o_mine, w_o_other], axis=0),
        NN,
    ).astype(bf16)
    d_all = jnp.concatenate([d_query[:rows], core_swap(d_query[rows:]), d_own, core_swap(d_next)], axis=1)
    input_grad = dot(d_all, w_all, NT).astype(bf16)
    terms = after(lax.all_to_all(jnp.broadcast_to(share[None], (8, 192, E)), RING, 0, 0), layer_out, input_grad)
    terms = terms.astype(f32)
    kv_sum = jnp.sum(terms[:, :96], axis=0)
    qo_sum = (terms[:4, 96:] + terms[4:, 96:]).reshape(384, E)
    final = lax.optimization_barrier(jnp.concatenate([kv_sum, qo_sum], axis=0).astype(bf16))
    query_grad, key_grad, value_grad, output_grad = unpack(scalar, final, core_swap(final))

    return (layer_out[None], input_grad[None], query_grad, key_grad, value_grad, output_grad)


def solution(mesh):
    split = Mesh(mesh.devices.reshape(2, 4, 2, 4, 4), (ZL, Y, CORE, X, ZH))
    seq = (ZL, Y, CORE)
    return jax.shard_map(
        shards,
        mesh=split,
        in_specs=(
            P(FSDP, seq, None),
            P(FSDP, None),
            P(FSDP, None),
            P(FSDP, None),
            P(FSDP, None),
            P(FSDP, seq, None),
        ),
        out_specs=(
            P(FSDP, seq, None),
            P(FSDP, seq, None),
            P(FSDP, None),
            P(FSDP, None),
            P(FSDP, None),
            P(FSDP, None),
        ),
        check_vma=False,
    )
```
